512 devices in a mesh: prow: 16 (over z, core), pcol: 32 (over y, x).
Axes of the slice: x: 4, y: 8, z: 8, core: 2. Of those that a mesh axis runs over, the one named last changes fastest.
Arguments:
- covariance: float32 [2, 16, 512, 1, 32, 512], P(None, 'prow', None, None, 'pcol'), may hold values from 0 to 5, as said below
- observations: float32 [2, 16, 512, 256], P(None, 'prow', 'pcol'), may hold values from -6 to 6
Outputs:
- factor: float32 [2, 16, 512, 1, 32, 512], P(None, 'prow', None, None, 'pcol')
- reduced: float32 [2, 16, 512, 256], P(None, 'prow', 'pcol')
The draws below stay inside these ranges and needn't reach their ends.
Inputs may be any that keep to these rules, and one draw needn't show every extreme that they name: Symmetric positive definite: a Matern covariance of smoothness 3/2 and range 0.1 between random points in the unit square, with a positive scale on each point and a positive nugget added on the diagonal.
All inputs are finite; a program needn't handle non-finite values.
Results may differ from the reference program's by a relative error of at most 0.0003.
Values sent between devices are 32-bit elements; how exact they have to be, the bound alone decides.
A program may use at most 64 MiB of HBM per device.

```python
import math
import jax
import jax.numpy as jnp
from jax import lax

B = 512
NRHS = 256
TC = 1
TR = 2
ORDER = 16384
N_PROW = 16
N_PCOL = 32


def draw_covariance(key, part):
    key = jax.random.fold_in(key, 7)
    point_key, scale_key, nugget_key = jax.random.split(key, 3)
    points = jax.random.uniform(point_key, (ORDER, 2), jnp.float32)
    scales = jnp.exp(jax.random.uniform(scale_key, (ORDER,), jnp.float32, -0.35, 0.35))
    nuggets = jax.random.uniform(nugget_key, (ORDER,), jnp.float32, 0.4, 0.8)
    reach = math.sqrt(3.0) / 0.1
    columns = jnp.arange(ORDER, dtype=jnp.int32)

    def tile_row(index):
        start = (index * B).astype(jnp.int32)
        near = lax.dynamic_slice_in_dim(points, start, B, 0)
        near_scale = lax.dynamic_slice_in_dim(scales, start, B, 0)
        near_nugget = lax.dynamic_slice_in_dim(nuggets, start, B, 0)
        delta_x = near[:, 0:1] - points[None, :, 0]
        delta_y = near[:, 1:2] - points[None, :, 1]
        distance = jnp.sqrt(delta_x * delta_x + delta_y * delta_y) * reach
        kernel = (1.0 + distance) * jnp.exp(-distance)
        same = (start + jnp.arange(B, dtype=jnp.int32))[:, None] == columns[None, :]
        return near_scale[:, None] * scales[None, :] * kernel + jnp.where(same, near_nugget[:, None], 0.0)
    matrix = lax.map(tile_row, jnp.arange(ORDER // B, dtype=jnp.int32))
    return matrix.reshape(TR, N_PROW, B, TC, N_PCOL, B)


def block_levels(rng, shape, pieces, smallest, largest):
    loudness, own = 1.0, jax.random.fold_in(rng, 6)
    for dim, shards_of in pieces:
        steps = jnp.exp(jax.random.uniform(jax.random.fold_in(own, dim), (shards_of,), jnp.float32, smallest / len(pieces), largest / len(pieces)))
        loudness = loudness * jnp.repeat(steps, shape[dim] // shards_of).reshape([-1 if axis == dim else 1 for axis in range(len(shape))])
    return loudness


def noise(key, extent, width, bound, pieces=(), kind=jnp.bfloat16):
    array = width * jax.random.normal(key, extent, jnp.float32)
    if pieces:
        array = array * block_levels(key, extent, pieces, -0.22, 0.18)
    return jnp.clip(array, -bound, bound).astype(kind)


def setup_inputs(seed: int = 0) -> dict:
    arg_keys = jax.random.split(jax.random.key(seed), 3)
    return {
        "covariance": draw_covariance(jax.random.fold_in(arg_keys[2], 71), 0),
        "observations": noise(arg_keys[1], (TR, N_PROW, B, NRHS), 1.0, 6.0, ((1, 16), (2, 32)), jnp.float32),
    }


precision_mode = lax.Precision.HIGHEST

def reference(covariance, observations):
    matrix = covariance.reshape(ORDER, ORDER)
    values = observations.reshape(ORDER, NRHS)
    tile_of = jnp.arange(ORDER, dtype=jnp.int32) // B
    for current in range(2):
        first = current * B
        diag_factor = jnp.linalg.cholesky(matrix[first:first + B, first:first + B])
        column = matrix[:, first:first + B]
        column_factor = jax.scipy.linalg.solve_triangular(diag_factor, column.T, lower=True).T
        column_factor = jnp.where((tile_of < current)[:, None], 0.0, column_factor)
        column_factor = column_factor.at[first:first + B].set(diag_factor)

        def update_column(index, whole):
            start = (index * B).astype(jnp.int32)
            block_cols = lax.dynamic_slice_in_dim(whole, start, B, 1)
            partner = lax.dynamic_slice_in_dim(column_factor, start, B, 0)
            product = jnp.dot(column_factor.astype(jnp.float32), partner.T.astype(jnp.float32), precision=precision_mode, preferred_element_type=jnp.float32)
            block_cols = block_cols - jnp.where((tile_of >= index)[:, None], product, 0.0)
            return lax.dynamic_update_slice_in_dim(whole, block_cols, start, 1)
        matrix = lax.fori_loop(current + 1, ORDER // B, update_column, matrix)
        matrix = matrix.at[:, first:first + B].set(column_factor)
        solved = jax.scipy.linalg.solve_triangular(diag_factor, values[first:first + B], lower=True)
        change = jnp.dot(column_factor.astype(jnp.float32), solved.astype(jnp.float32), precision=precision_mode, preferred_element_type=jnp.float32)
        values = jnp.where((tile_of > current)[:, None], values - change, values)
        values = values.at[first:first + B].set(solved)
    keeping = tile_of[:, None] >= tile_of[None, :]
    matrix = jnp.where(keeping, matrix, 0.0)
    return (matrix.reshape(covariance.shape), values.reshape(observations.shape))
```

```python
import functools

import jax
import jax.numpy as jnp
from jax import lax
from jax.experimental import pallas as pl
from jax.experimental.pallas import tpu as pltpu
from jax.sharding import PartitionSpec as P

HIGHEST = lax.Precision.HIGHEST
HIGH = lax.Precision.HIGH
MESH = pl.DeviceIdType.MESH
ROWS8 = 8
NY, NX, NZ = 8, 4, 8


def tn(a, b, precision=HIGH):
    return lax.dot_general(
        a, b, (((0,), (0,)), ((), ())), precision=precision, preferred_element_type=jnp.float32
    )


def nt(a, b, precision=HIGH):
    return lax.dot_general(
        a, b, (((1,), (1,)), ((), ())), precision=precision, preferred_element_type=jnp.float32
    )


def nn(a, b, precision=HIGH):
    return lax.dot_general(
        a, b, (((1,), (0,)), ((), ())), precision=precision, preferred_element_type=jnp.float32
    )


def lane_copy(x, i):
    return jnp.broadcast_to(x[:, i : i + 1], (8, 128))


def row_copy(ref, row):
    return ref[pl.ds(row, 8, stride=0), :]


def factor128(block, inv_ref, row_ref, col_ref, window=2, ahead=2, precision=HIGHEST):
    sub = lax.broadcasted_iota(jnp.int32, (8, 128), 0)
    lane = lax.broadcasted_iota(jnp.int32, (8, 128), 1)
    count = 16
    tiles = [block[8 * i : 8 * i + 8, :] for i in range(count)]
    group = []
    for t in range(count):
        g = t // window
        here = (lane >= 8 * t) & (lane < 8 * t + 8)
        row_ref[8 * t : 8 * t + 8, :] = tiles[t]
        rows = [
            jnp.where(here, jnp.where(lane == 8 * t + i, 1.0, 0.0), row_copy(row_ref, 8 * t + i))
            for i in range(8)
        ]
        base = 64 * (t % 2)
        for j in range(8):
            col_ref[base + 8 * j : base + 8 * j + 8, :] = lane_copy(tiles[t], 8 * t + j)
        s = {(i, k): row_copy(col_ref, base + 8 * i + k) for i in range(8) for k in range(i, 8)}
        later = list(range(t + 1, min((g + 1) * window + ahead, count)))
        cols = {q: [lane_copy(tiles[q], 8 * t + j) for j in range(8)] for q in later}
        rest = {q: jnp.where(here, 0.0, tiles[q]) for q in later}
        for j in range(8):
            r = lax.rsqrt(s[j, j])
            u = {k: s[j, k] * r for k in range(j + 1, 8)}
            for i in range(j + 1, 8):
                for k in range(i, 8):
                    s[i, k] = s[i, k] - u[i] * u[k]
            rows[j] = rows[j] * r
            for i in range(j + 1, 8):
                rows[i] = rows[i] - u[i] * rows[j]
            for q in later:
                m = cols[q][j] * r
                for k in range(j + 1, 8):
                    cols[q][k] = cols[q][k] - m * u[k]
                rest[q] = rest[q] - m * rows[j]
        done = rows[0]
        for i in range(1, 8):
            done = jnp.where(sub == i, rows[i], done)
        inv_ref[8 * t : 8 * t + 8, :] = jnp.where(lane < 8 * t + 8, done, 0.0)
        group.append(done)
        for q in later:
            tiles[q] = rest[q]
        if t % window == window - 1:
            first = (g + 1) * window + ahead
            if first < count:
                inside = (lane >= 8 * g * window) & (lane < 8 * (g + 1) * window)
                right = [
                    jnp.where(
                        (lane >= 8 * (g * window + a + 1)) & (lane < 8 * (g + 1) * window),
                        0.0,
                        group[a],
                    )
                    for a in range(window)
                ]
                v = tn(jnp.concatenate(group, 0), jnp.concatenate(right, 0), precision)
                for i in range(first, count):
                    tiles[i] = jnp.where(inside, 0.0, tiles[i]) - v[8 * i : 8 * i + 8, :]
            group = []


def compute_kernel(
    lead_ref, cross_ref, panel_ref, cov_ref, obs_ref, out_ref, red_ref,
    g, x, tile, mine, inv_a, inv_b, inv2, row_ref, col_ref, sems,
):
    p = lax.axis_index("prow")
    c = lax.axis_index("pcol")
    lead_in = pltpu.make_async_copy(lead_ref, g.at[:, 0:1280], sems.at[0])
    cross_in = pltpu.make_async_copy(cross_ref, g.at[:, 1280:1792], sems.at[1])
    panel_in = pltpu.make_async_copy(panel_ref, x, sems.at[2])
    tile_in = pltpu.make_async_copy(cov_ref, tile, sems.at[3])
    lead_in.start()
    cross_in.start()
    panel_in.start()
    tile_in.start()
    lead_in.wait()
    for big in range(4):
        lo, mid, hi = 256 * big, 256 * big + 128, 256 * big + 256
        factor128(g[lo:mid, lo:mid], inv_a, row_ref, col_ref)
        ia = inv_a[...]
        u = nn(ia, g[lo:mid, mid:hi], HIGHEST)
        factor128(g[mid:hi, mid:hi] - tn(u, u, HIGHEST), inv_b, row_ref, col_ref)
        ib = inv_b[...]
        inv2[0:128, 0:128] = ia
        inv2[0:128, 128:256] = jnp.zeros((128, 128), jnp.float32)
        inv2[128:256, 0:128] = -nn(ib, tn(u, ia, HIGHEST), HIGHEST)
        inv2[128:256, 128:256] = ib
        if big == 0:
            cross_in.wait()
            panel_in.wait()
        inv = inv2[...]
        for start in range(hi, 1792, 256):
            g[lo:hi, start : start + 256] = nn(inv, g[lo:hi, start : start + 256])
        for row in range(hi, 1024, 256):
            left = g[lo:hi, row : row + 256]
            for start in range(row, 1792, 256):
                g[row : row + 256, start : start + 256] -= tn(left, g[lo:hi, start : start + 256])

        @pl.loop(0, 4)
        def _(i):
            at = pl.ds(pl.multiple_of(i * 256, 256), 256)
            solved = nt(x[at, lo:hi], inv2[...])
            x[at, lo:hi] = solved
            for start in range(hi, 1024, 256):
                x[at, start : start + 256] -= nn(solved, g[lo:hi, start : start + 256])

    tile_in.wait()
    sub = lax.broadcasted_iota(jnp.int32, (256, 512), 0)
    lane = lax.broadcasted_iota(jnp.int32, (256, 512), 1)

    @pl.loop(0, 4)
    def _(i):
        at = pl.ds(pl.multiple_of(i * 256, 256), 256)
        below = p + 16 * (i // 2)

        @pl.when(c <= 1)
        def _():
            half = jnp.where(c == 0, x[at, 0:512], x[at, 512:1024])
            row = sub + 256 * (i % 2)
            keep = (below > c) | ((below == c) & (row >= lane))
            tile[at, :] = jnp.where(keep, half, 0.0)

        @pl.when((c > 1) & (below >= c))
        def _():
            tile[at, :] -= nn(x[at, :], g[:, 1280:1792])

        @pl.when((c > 1) & (below < c))
        def _():
            tile[at, :] = jnp.zeros((256, 512), jnp.float32)

    tile_out = pltpu.make_async_copy(tile, out_ref, sems.at[4])
    tile_out.start()
    y = g[:, 1024:1280]
    for r in range(2):
        at = pl.ds(pl.multiple_of(512 * r + 16 * c, 16), 16)
        strip = x[at, :]
        if r == 1:
            mine[...] = obs_ref[1] - nn(strip, y)
            red_ref[1] = mine[...]
        else:
            base = obs_ref[0]

            @pl.when(p > 1)
            def _():
                red_ref[0] = base - nn(strip, y)

            @pl.when(p <= 1)
            def _():
                rows = pl.ds(pl.multiple_of(512 * p + 16 * c, 16), 16)
                red_ref[0] = g[rows, 1024:1280]

    tile_out.wait()


def compute(lead, cross, panel, cov, obs):
    any_space = pl.BlockSpec(memory_space=pl.ANY)
    vmem = pl.BlockSpec(memory_space=pltpu.VMEM)
    return pl.pallas_call(
        compute_kernel,
        out_shape=[
            jax.ShapeDtypeStruct((1024, 512), jnp.float32),
            jax.ShapeDtypeStruct((2, 16, 256), jnp.float32),
        ],
        in_specs=[any_space, any_space, any_space, any_space, vmem],
        out_specs=[any_space, vmem],
        scratch_shapes=[
            pltpu.VMEM((1024, 1792), jnp.float32),
            pltpu.VMEM((1024, 1024), jnp.float32),
            pltpu.VMEM((1024, 512), jnp.float32),
            pltpu.VMEM((16, 256), jnp.float32),
            pltpu.VMEM((128, 128), jnp.float32),
            pltpu.VMEM((128, 128), jnp.float32),
            pltpu.VMEM((256, 256), jnp.float32),
            pltpu.VMEM((128, 128), jnp.float32),
            pltpu.VMEM((128, 128), jnp.float32),
            pltpu.SemaphoreType.DMA((5,)),
        ],
        compiler_params=pltpu.CompilerParams(vmem_limit_bytes=56 * 1024 * 1024),
    )(lead, cross, panel, cov, obs)


class Mover:
    def __init__(self, send_sems, recv_sems):
        self.send_sems, self.recv_sems, self.used, self.sent = send_sems, recv_sems, 0, []

    def copy(self, src, dst, device):
        slot = self.used
        self.used += 1
        return pltpu.make_async_remote_copy(
            src_ref=src, dst_ref=dst, send_sem=self.send_sems.at[slot],
            recv_sem=self.recv_sems.at[slot], device_id=device, device_id_type=MESH,
        )


def one_way(mover, view, size, me, step, device):
    half = 0 if step == 1 else 1
    for hop in range(1, size // 2 + 1):
        part = half if hop == size // 2 else None
        block = lax.rem(me - step * (hop - 1) + 2 * size, size)
        ref = view(block, part)
        copy = mover.copy(ref, ref, device)
        copy.start()
        mover.sent.append(copy)
        yield
        copy.wait_recv()


def both_ways(mover, view, size, me, ahead, behind):
    jobs = [one_way(mover, view, size, me, 1, ahead), one_way(mover, view, size, me, -1, behind)]
    while jobs:
        for job in list(jobs):
            try:
                next(job)
                yield
            except StopIteration:
                jobs.remove(job)


def move_kernel(cov_ref, obs_ref, panel, lead, cross, send_sems, recv_sems, wide_sems, local_sems):
    p = lax.axis_index("prow")
    c = lax.axis_index("pcol")
    z, core = p // 2, lax.rem(p, 2)
    y, x = c // NX, lax.rem(c, NX)

    def at(zz, yy, xx, cc=core):
        return (2 * zz + cc, yy * NX + xx)

    def ring(v, d, n):
        return lax.rem(v + d + n, n)

    xn, xp = at(z, y, ring(x, 1, NX)), at(z, y, ring(x, -1, NX))
    yn, yp = at(z, ring(y, 1, NY), x), at(z, ring(y, -1, NY), x)
    zn, zp = at(ring(z, 1, NZ), y, x), at(ring(z, -1, NZ), y, x)
    sibling = at(z, y, x, 1 - core)

    barrier = pltpu.get_barrier_semaphore()

    @pl.loop(1, 32)
    def _(d):
        pl.semaphore_signal(barrier, inc=1, device_id=(p, lax.rem(c + d, 32)), device_id_type=MESH)

    @pl.loop(1, 16)
    def _(d):
        pl.semaphore_signal(barrier, inc=1, device_id=(lax.rem(p + d, 16), c), device_id_type=MESH)

    pl.semaphore_wait(barrier, 46)

    mover = Mover(send_sems, recv_sems)

    def share(col, to):
        return (
            cov_ref.at[:, pl.ds(pl.multiple_of(to * 16, 16), 16), :],
            panel.at[:, to // NX, lax.rem(to, NX), :, 512 * col : 512 * col + 512],
        )

    def share_copy(col, to):
        src, dst = share(col, to)
        return pltpu.make_async_remote_copy(
            src_ref=src, dst_ref=dst, send_sem=wide_sems.at[0], recv_sem=wide_sems.at[1 + col],
            device_id=(p, to), device_id_type=MESH,
        )

    for col in range(2):

        @pl.when(c == col)
        def _():
            @pl.loop(1, 32)
            def _(d):
                share_copy(col, lax.rem(c + d, 32)).start()

            src, dst = share(col, c)
            own = pltpu.make_async_copy(src, dst, local_sems.at[0])
            own.start()
            own.wait()

    def slab(to):
        ref = cov_ref.at[0, pl.ds(pl.multiple_of(to * 64, 64), 64), :]
        return ref, cross.at[core, to]

    def slab_copy(to):
        src, dst = slab(to)
        return pltpu.make_async_remote_copy(
            src_ref=src, dst_ref=dst, send_sem=wide_sems.at[3], recv_sem=wide_sems.at[4],
            device_id=at(to, y, x), device_id_type=MESH,
        )

    def rhs_copy(to):
        return pltpu.make_async_remote_copy(
            src_ref=obs_ref.at[0], dst_ref=lead.at[core, y, x, :, 1024:1280],
            send_sem=wide_sems.at[5], recv_sem=wide_sems.at[6],
            device_id=at(to, y, x), device_id_type=MESH,
        )

    def lead_copy(to):
        return pltpu.make_async_remote_copy(
            src_ref=panel.at[0, y, x], dst_ref=lead.at[core, y, x, :, 0:1024],
            send_sem=wide_sems.at[7], recv_sem=wide_sems.at[8],
            device_id=at(to, y, x), device_id_type=MESH,
        )

    @pl.when(z == 0)
    def _():
        @pl.loop(1, NZ)
        def _(d):
            rhs_copy(d).start()
            slab_copy(d).start()

        src, dst = slab(0)
        own = pltpu.make_async_copy(src, dst, local_sems.at[1])
        own.start()
        own_rhs = pltpu.make_async_copy(
            obs_ref.at[0], lead.at[core, y, x, :, 1024:1280], local_sems.at[2]
        )
        own_rhs.start()
        own.wait()
        own_rhs.wait()

    for col in range(2):

        @pl.when(c != col)
        def _():
            share_copy(col, c).wait_recv()

    @pl.when(z == 0)
    def _():
        @pl.loop(1, NZ)
        def _(d):
            lead_copy(d).start()

        own = pltpu.make_async_copy(
            panel.at[0, y, x], lead.at[core, y, x, :, 0:1024], local_sems.at[3]
        )
        own.start()
        own.wait()

    def rows_of(ref, part, size):
        return ref if part is None else ref.at[pl.ds(part * size // 2, size // 2)]

    def y_then_x(where):
        def y_view(block, part):
            return rows_of(where(block, x), part, 16)

        def x_view(block, part):
            return where(slice(0, NY) if part is None else slice(4 * part, 4 * part + 4), block)

        yield from both_ways(mover, y_view, NY, y, yn, yp)
        yield from both_ways(mover, x_view, NX, x, xn, xp)

    def x_then_y(where):
        def x_view(block, part):
            return rows_of(where(y, block), part, 16)

        def y_view(block, part):
            return where(block, slice(0, NX) if part is None else slice(2 * part, 2 * part + 2))

        yield from both_ways(mover, x_view, NX, x, xn, xp)
        yield from both_ways(mover, y_view, NY, y, yn, yp)

    def lead_job():
        yield

        @pl.when(z != 0)
        def _():
            rhs_copy(0).wait_recv()
            lead_copy(0).wait_recv()

        yield from y_then_x(lambda yy, xx: lead.at[core, yy, xx])
        copy = mover.copy(lead.at[core], lead.at[core], sibling)
        copy.start()
        mover.sent.append(copy)
        yield
        copy.wait_recv()

    def cross_job():
        yield

        @pl.when(z != 0)
        def _():
            slab_copy(0).wait_recv()

        def view(block, part):
            return rows_of(cross.at[core, block], part, 64)

        yield from both_ways(mover, view, NZ, z, zn, zp)
        copy = mover.copy(cross.at[core], cross.at[core], sibling)
        copy.start()
        mover.sent.append(copy)
        yield
        copy.wait_recv()

    jobs = [
        x_then_y(lambda yy, xx: panel.at[1, yy, xx]),
        y_then_x(lambda yy, xx: panel.at[0, yy, xx]),
        cross_job(),
        lead_job(),
    ]
    while jobs:
        for job in list(jobs):
            try:
                next(job)
            except StopIteration:
                jobs.remove(job)
    for copy in mover.sent:
        copy.wait_send()

    for col in range(2):

        @pl.when(c == col)
        def _():
            @pl.loop(1, 32)
            def _(d):
                share_copy(col, lax.rem(c + d, 32)).wait_send()

    @pl.when(z == 0)
    def _():
        @pl.loop(1, NZ)
        def _(d):
            rhs_copy(d).wait_send()
            slab_copy(d).wait_send()
            lead_copy(d).wait_send()


def move(cov, obs):
    any_space = pl.BlockSpec(memory_space=pl.ANY)
    return pl.pallas_call(
        move_kernel,
        out_shape=[
            jax.ShapeDtypeStruct((2, NY, NX, 16, 1024), jnp.float32),
            jax.ShapeDtypeStruct((2, NY, NX, 16, 1280), jnp.float32),
            jax.ShapeDtypeStruct((2, NZ, 64, 512), jnp.float32),
        ],
        in_specs=[any_space] * 2,
        out_specs=[any_space] * 3,
        scratch_shapes=[
            pltpu.SemaphoreType.DMA((64,)),
            pltpu.SemaphoreType.DMA((64,)),
            pltpu.SemaphoreType.DMA((9,)),
            pltpu.SemaphoreType.DMA((4,)),
        ],
        compiler_params=pltpu.CompilerParams(collective_id=0, has_side_effects=True),
    )(cov, obs)


def body(covariance, observations):
    cov = covariance.reshape(2, 512, 512)
    obs = observations.reshape(2, 16, 256)
    panel, lead, cross = move(cov, obs)
    factor, reduced = compute(
        lead.reshape(1024, 1280), cross.reshape(1024, 512), panel.reshape(1024, 1024),
        cov.reshape(1024, 512), obs,
    )
    return factor.reshape(covariance.shape), reduced.reshape(observations.shape)


def solution(mesh):
    return jax.shard_map(
        body,
        mesh=mesh,
        in_specs=(P(None, "prow", None, None, "pcol", None), P(None, "prow", "pcol", None)),
        out_specs=(P(None, "prow", None, None, "pcol", None), P(None, "prow", "pcol", None)),
        check_vma=False,
    )
```

```python
import functools

import jax
import jax.numpy as jnp
from jax import lax
from jax.experimental import pallas as pl
from jax.experimental.pallas import tpu as pltpu
from jax.sharding import PartitionSpec as P

HIGHEST = lax.Precision.HIGHEST
HIGH = lax.Precision.HIGH
MESH = pl.DeviceIdType.MESH
ROWS8 = 8
NY, NX, NZ = 8, 4, 8


def tn(a, b, precision=HIGH):
    return lax.dot_general(
        a, b, (((0,), (0,)), ((), ())), precision=precision, preferred_element_type=jnp.float32
    )


def nt(a, b, precision=HIGH):
    return lax.dot_general(
        a, b, (((1,), (1,)), ((), ())), precision=precision, preferred_element_type=jnp.float32
    )


def nn(a, b, precision=HIGH):
    return lax.dot_general(
        a, b, (((1,), (0,)), ((), ())), precision=precision, preferred_element_type=jnp.float32
    )


def lane_copy(x, i):
    return jnp.broadcast_to(x[:, i : i + 1], (8, 128))


def row_copy(ref, row):
    return ref[pl.ds(row, 8, stride=0), :]


def factor128(block, inv_ref, row_ref, col_ref, window=2, ahead=2, precision=HIGHEST):
    sub = lax.broadcasted_iota(jnp.int32, (8, 128), 0)
    lane = lax.broadcasted_iota(jnp.int32, (8, 128), 1)
    count = 16
    tiles = [block[8 * i : 8 * i + 8, :] for i in range(count)]
    group = []
    for t in range(count):
        g = t // window
        here = (lane >= 8 * t) & (lane < 8 * t + 8)
        row_ref[8 * t : 8 * t + 8, :] = tiles[t]
        rows = [
            jnp.where(here, jnp.where(lane == 8 * t + i, 1.0, 0.0), row_copy(row_ref, 8 * t + i))
            for i in range(8)
        ]
        base = 64 * (t % 2)
        for j in range(8):
            col_ref[base + 8 * j : base + 8 * j + 8, :] = lane_copy(tiles[t], 8 * t + j)
        s = {(i, k): row_copy(col_ref, base + 8 * i + k) for i in range(8) for k in range(i, 8)}
        later = list(range(t + 1, min((g + 1) * window + ahead, count)))
        cols = {q: [lane_copy(tiles[q], 8 * t + j) for j in range(8)] for q in later}
        rest = {q: jnp.where(here, 0.0, tiles[q]) for q in later}
        for j in range(8):
            r = lax.rsqrt(s[j, j])
            u = {k: s[j, k] * r for k in range(j + 1, 8)}
            for i in range(j + 1, 8):
                for k in range(i, 8):
                    s[i, k] = s[i, k] - u[i] * u[k]
            rows[j] = rows[j] * r
            for i in range(j + 1, 8):
                rows[i] = rows[i] - u[i] * rows[j]
            for q in later:
                m = cols[q][j] * r
                for k in range(j + 1, 8):
                    cols[q][k] = cols[q][k] - m * u[k]
                rest[q] = rest[q] - m * rows[j]
        done = rows[0]
        for i in range(1, 8):
            done = jnp.where(sub == i, rows[i], done)
        inv_ref[8 * t : 8 * t + 8, :] = jnp.where(lane < 8 * t + 8, done, 0.0)
        group.append(done)
        for q in later:
            tiles[q] = rest[q]
        if t % window == window - 1:
            first = (g + 1) * window + ahead
            if first < count:
                inside = (lane >= 8 * g * window) & (lane < 8 * (g + 1) * window)
                right = [
                    jnp.where(
                        (lane >= 8 * (g * window + a + 1)) & (lane < 8 * (g + 1) * window),
                        0.0,
                        group[a],
                    )
                    for a in range(window)
                ]
                v = tn(jnp.concatenate(group, 0), jnp.concatenate(right, 0), precision)
                for i in range(first, count):
                    tiles[i] = jnp.where(inside, 0.0, tiles[i]) - v[8 * i : 8 * i + 8, :]
            group = []


class Mover:
    def __init__(self, send_sems, recv_sems):
        self.send_sems, self.recv_sems, self.used, self.sent = send_sems, recv_sems, 0, []

    def copy(self, src, dst, device):
        slot = self.used
        self.used += 1

        def build():
            return pltpu.make_async_remote_copy(
                src_ref=src(), dst_ref=dst(), send_sem=self.send_sems.at[slot],
                recv_sem=self.recv_sems.at[slot], device_id=device, device_id_type=MESH,
            )

        return build


def all_to_all_peers(mover, views, size, me, device, active=None):
    copies = [
        mover.copy(functools.partial(view, me), functools.partial(view, me), device(lax.rem(me + d, size)))
        for view in views
        for d in range(1, size)
    ]

    def start():
        for copy in copies:
            copy().start()

    def wait():
        for copy in copies:
            copy().wait_recv()

    def end():
        for copy in copies:
            copy().wait_send()

    def guarded(f):
        if active is None:
            return f
        return lambda: pl.when(active)(f)

    mover.sent.append(guarded(end))
    return guarded(start), guarded(wait)


def ring(mover, view, size, me, device):
    steps = []
    for hop in range(1, size // 2 + 1):
        copies = []
        for side, step in ((0, 1), (1, -1)):
            part = side if hop == size // 2 else None
            block = lax.rem(me - step * (hop - 1) + 2 * size, size)
            ref = functools.partial(view, block, part)
            copies.append(mover.copy(ref, ref, device(lax.rem(me + step + size, size))))

        def start(copies=copies):
            for copy in copies:
                copy().start()

        def wait(copies=copies):
            for copy in copies:
                copy().wait_recv()

        def end(copies=copies):
            for copy in copies:
                copy().wait_send()

        mover.sent.append(end)
        steps.append((start, wait))
    return steps


def move_kernel(
    cov_ref, obs_ref, panel, rhs, cross, upper, inverses,
    lead, work, row_ref, col_ref, send_sems, recv_sems, wide_sems, local_sems,
):
    p = lax.axis_index("prow")
    c = lax.axis_index("pcol")
    z, core = p // 2, lax.rem(p, 2)
    y, x = c // NX, lax.rem(c, NX)

    def at(zz, yy, xx, cc=core):
        return (2 * zz + cc, yy * NX + xx)

    def x_device(v):
        return at(z, y, v)

    def y_device(v):
        return at(z, v, x)

    def z_device(v):
        return at(v, y, x)

    sibling = at(z, y, x, 1 - core)

    barrier = pltpu.get_barrier_semaphore()

    def greet(device):
        pl.semaphore_signal(barrier, inc=1, device_id=device, device_id_type=MESH)

    for d in range(1, NY):
        greet(y_device(lax.rem(y + d, NY)))
    for d in range(1, NX):
        greet(x_device(lax.rem(x + d, NX)))
    for d in range(1, NZ):
        greet(z_device(lax.rem(z + d, NZ)))
    greet(sibling)
    for col in range(2):

        @pl.when(c == col)
        def _():
            @pl.loop(1, 32)
            def _(d):
                greet((p, lax.rem(c + d, 32)))

        @pl.when(c != col)
        def _():
            greet((p, col))

    others = NY + NX + NZ - 2
    pl.semaphore_wait(
        barrier,
        others + jnp.where(c != 0, 1, 0) + jnp.where(c != 1, 1, 0) + jnp.where(c <= 1, 31, 0),
    )

    mover = Mover(send_sems, recv_sems)

    def remote(src, dst, send, recv, device):
        return pltpu.make_async_remote_copy(
            src_ref=src, dst_ref=dst, send_sem=wide_sems.at[send], recv_sem=wide_sems.at[recv],
            device_id=device, device_id_type=MESH,
        )

    def local(src, dst, slot):
        return pltpu.make_async_copy(src, dst, local_sems.at[slot])

    def rows16(ref, to):
        return ref.at[pl.ds(pl.multiple_of(to * 16, 16), 16), :]

    def lead_share(half, to):
        dst = lead.at[core, to // NX, lax.rem(to, NX), :, 512 * half : 512 * half + 512]
        return remote(rows16(cov_ref.at[0], to), dst, 2 * half, 2 * half + 1, (p, to))

    def lead_sender(half):
        return (c == half) & ((p == 0) if half == 0 else (z == 0))

    def lead_plane(half):
        return (p == 0) if half == 0 else (z == 0)

    def start_lead(half):
        @pl.when(lead_sender(half))
        def _():
            @pl.loop(1, 32)
            def _(d):
                lead_share(half, lax.rem(c + d, 32)).start()

            own = local(
                rows16(cov_ref.at[0], c), lead.at[core, y, x, :, 512 * half : 512 * half + 512], half
            )
            own.start()
            own.wait()

    def end_lead(half):
        @pl.when(lead_sender(half))
        def _():
            @pl.loop(1, 32)
            def _(d):
                lead_share(half, lax.rem(c + d, 32)).wait_send()

    def wait_lead(half):
        @pl.when(lead_plane(half) & (c != half))
        def _():
            lead_share(half, c).wait_recv()

    def lead_down(half, to):
        ref = lead.at[core, y, x, :, 512 * half : 512 * half + 512]
        return remote(ref, ref, 4 + 2 * half, 5 + 2 * half, z_device(to))

    def on_lead(half, condition):
        return (condition & (core == 0)) if half == 0 else condition

    def start_down(half):
        @pl.when(on_lead(half, z == 0))
        def _():
            @pl.loop(1, NZ)
            def _(d):
                lead_down(half, d).start()

    def wait_down(half):
        @pl.when(on_lead(half, z != 0))
        def _():
            lead_down(half, 0).wait_recv()

    def end_down(half):
        @pl.when(on_lead(half, z == 0))
        def _():
            @pl.loop(1, NZ)
            def _(d):
                lead_down(half, d).wait_send()

    def share(col, to):
        return (
            cov_ref.at[:, pl.ds(pl.multiple_of(to * 16, 16), 16), :],
            panel.at[:, to // NX, lax.rem(to, NX), :, 512 * col : 512 * col + 512],
        )

    def share_copy(col, to):
        src, dst = share(col, to)
        return remote(src, dst, 8, 9 + col, (p, to))

    def slab_copy(to):
        src = cov_ref.at[0, pl.ds(pl.multiple_of(to * 64, 64), 64), :]
        return remote(src, cross.at[core, to], 11, 12, z_device(to))

    def rhs_copy(to):
        return remote(obs_ref.at[0], rhs.at[core, y, x], 13, 14, z_device(to))

    start_lead(0)
    start_lead(1)

    @pl.when(z == 0)
    def _():
        @pl.loop(1, NZ)
        def _(d):
            rhs_copy(d).start()

        own = local(obs_ref.at[0], rhs.at[core, y, x], 2)
        own.start()
        own.wait()

    end_lead(0)
    end_lead(1)
    for col in range(2):

        @pl.when(c == col)
        def _():
            @pl.loop(1, 32)
            def _(d):
                share_copy(col, lax.rem(c + d, 32)).start()

            src, dst = share(col, c)
            own = local(src, dst, 3)
            own.start()
            own.wait()

    def lead_y(half):
        return lambda block: lead.at[core, block, x, :, 512 * half : 512 * half + 512]

    def lead_x(half):
        return lambda block: lead.at[core, :, block, :, 512 * half : 512 * half + 512]

    def rhs_y(block):
        return rhs.at[core, block, x]

    def rhs_x(block):
        return rhs.at[core, :, block]

    def peers(views, size, me, device, active=None):
        return all_to_all_peers(mover, views, size, me, device, active)

    first_slots = mover.used
    mover.used += NY

    def first_y(d):
        ref = lead_y(0)(y)
        return pltpu.make_async_remote_copy(
            src_ref=ref, dst_ref=ref, send_sem=send_sems.at[first_slots + d],
            recv_sem=recv_sems.at[first_slots + y], device_id=y_device(lax.rem(y + d, NY)),
            device_id_type=MESH,
        )

    def first_y_wait(v):
        ref = lead_y(0)(v)
        return pltpu.make_async_remote_copy(
            src_ref=ref, dst_ref=ref, send_sem=send_sems.at[first_slots],
            recv_sem=recv_sems.at[first_slots + v], device_id=y_device(v), device_id_type=MESH,
        )

    def pair_rows(q, block):
        return lead.at[0, 2 * q : 2 * q + 2, block, :, 0:512]

    first_x = [
        [
            mover.copy(
                functools.partial(pair_rows, q, x), functools.partial(pair_rows, q, x),
                x_device(lax.rem(x + d, NX)),
            )
            for d in range(1, NX)
        ]
        for q in range(4)
    ]
    first_pair = [
        mover.copy(
            functools.partial(pair_rows, q, slice(0, NX)),
            functools.partial(pair_rows, q, slice(0, NX)), sibling,
        )
        for q in range(4)
    ]

    def y_arrived(q):
        @pl.when(core == 0)
        def _():
            for v in (2 * q, 2 * q + 1):

                @pl.when(y != v)
                def _():
                    first_y_wait(v).wait_recv()

            for copy in first_x[q]:
                copy().start()

    def x_arrived(q):
        @pl.when(core == 0)
        def _():
            for copy in first_x[q]:
                copy().wait_recv()
            first_pair[q]().start()

    def pair_arrived(q):
        @pl.when(core == 1)
        def _():
            first_pair[q]().wait_recv()

    def whole_or_half(view):
        return lambda block, part: view(
            slice(0, NY) if part is None else slice(4 * part, 4 * part + 4), block
        )

    second_y = peers([lead_y(1), rhs_y], NY, y, y_device)
    second_x = ring(
        mover, whole_or_half(lambda rows, block: lead.at[core, rows, block, :, 512:1024]),
        NX, x, x_device,
    )
    rhs_ring = ring(
        mover, whole_or_half(lambda rows, block: rhs.at[core, rows, block]), NX, x, x_device
    )
    cross_z = peers([lambda block: cross.at[core, block]], NZ, z, z_device)
    low_y = peers([lambda block: panel.at[0, block, x]], NY, y, y_device)
    high_x = peers([lambda block: panel.at[1, y, block]], NX, x, x_device)
    low_x = ring(
        mover,
        lambda block, part: panel.at[
            0, slice(0, NY) if part is None else slice(4 * part, 4 * part + 4), block
        ],
        NX, x, x_device,
    )
    high_y = ring(
        mover,
        lambda block, part: panel.at[
            1, block, slice(0, NX) if part is None else slice(2 * part, 2 * part + 2)
        ],
        NY, y, y_device,
    )

    def to_sibling(view):
        build = mover.copy(view, view, sibling)
        mover.sent.append(lambda: build().wait_send())
        return lambda: build().start(), lambda: build().wait_recv()

    second_pair = to_sibling(lambda: lead.at[core, :, :, :, 512:1024])
    rhs_pair = to_sibling(lambda: rhs.at[core])
    cross_pair = to_sibling(lambda: cross.at[core])

    wait_lead(0)
    start_down(0)
    wait_lead(1)
    start_down(1)
    wait_down(0)

    @pl.when(core == 0)
    def _():
        for d in range(1, NY):
            first_y(d).start()

    @pl.when(z == 0)
    def _():
        @pl.loop(1, NZ)
        def _(d):
            slab_copy(d).start()

        own = local(cov_ref.at[0, 0:64, :], cross.at[core, 0], 4)
        own.start()
        own.wait()

    y_arrived(0)
    y_arrived(1)

    @pl.when(z != 0)
    def _():
        rhs_copy(0).wait_recv()

    wait_down(1)
    second_y[0]()
    y_arrived(2)
    y_arrived(3)
    x_arrived(0)
    x_arrived(1)
    for col in range(2):

        @pl.when(c != col)
        def _():
            share_copy(col, c).wait_recv()

    high_x[0]()
    low_y[0]()
    second_y[1]()
    second_x[0][0]()
    rhs_ring[0][0]()

    @pl.when(z != 0)
    def _():
        slab_copy(0).wait_recv()

    cross_z[0]()
    pair_arrived(0)

    def slot0():
        x_arrived(2)
        pair_arrived(1)
        high_x[1]()
        high_y[0][0]()
        second_x[0][1]()
        rhs_ring[0][1]()
        second_x[1][0]()
        rhs_ring[1][0]()

    def slot1():
        x_arrived(3)
        pair_arrived(2)
        low_y[1]()
        low_x[0][0]()
        second_x[1][1]()
        second_pair[0]()
        rhs_ring[1][1]()
        rhs_pair[0]()
        high_y[0][1]()
        high_y[1][0]()

    def slot2():
        pair_arrived(3)
        high_y[1][1]()
        high_y[2][0]()
        low_x[0][1]()
        low_x[1][0]()

    def slot3():
        second_pair[1]()

    def slot4():
        high_y[2][1]()
        high_y[3][0]()
        cross_z[1]()
        cross_pair[0]()

    def slot6():
        rhs_pair[1]()
        low_x[1][1]()
        high_y[3][1]()
        cross_pair[1]()

    slots = {0: slot0, 1: slot1, 2: slot2, 3: slot3, 4: slot4, 6: slot6}

    upper[...] = jnp.zeros((1024, 1024), jnp.float32)

    @pl.loop(0, 8)
    def _(a):
        at_row = pl.ds(pl.multiple_of(128 * lax.rem(a, 4), 128), 128)
        at_wide = pl.ds(pl.multiple_of(512 * (a // 4), 512), 512)
        at_upper = pl.ds(pl.multiple_of(128 * a, 128), 128)

        @pl.when(a < 4)
        def _():
            for i in range(8):
                work[pl.ds(pl.multiple_of(128 * a + 16 * i, 16), 16), :] = lead[
                    0, 2 * a + i // NX, i % NX, :, 0:512
                ]

        @pl.when(a == 4)
        def _():
            for i in range(32):
                upper[16 * i : 16 * i + 16, 512:1024] = lead[0, i // NX, i % NX, :, 512:1024]
                work[16 * i : 16 * i + 16, :] = lead[1, i // NX, i % NX, :, 512:1024]
            for k in range(4):
                rows = slice(128 * k, 128 * k + 128)
                if k:
                    upper[rows, 512:1024] -= tn(
                        upper[0 : 128 * k, rows], upper[0 : 128 * k, 512:1024], HIGHEST
                    )
                upper[rows, 512:1024] = nn(inverses[k], upper[rows, 512:1024], HIGHEST)

            @pl.loop(0, 4)
            def _(i):
                cut = pl.ds(pl.multiple_of(128 * i, 128), 128)
                left = upper[0:512, pl.ds(pl.multiple_of(512 + 128 * i, 128), 128)]
                work[cut, :] -= tn(left, upper[0:512, 512:1024], HIGHEST)

        work[at_row, :] -= tn(upper[at_wide, at_upper], upper[at_wide, at_wide], HIGHEST)
        factor128(work[at_row, at_row], inverses.at[a], row_ref, col_ref)
        upper[at_upper, at_wide] = nn(inverses[a], work[at_row, :], HIGHEST)
        for index, events in slots.items():
            pl.when(a == index)(events)

    for end in mover.sent:
        end()

    @pl.when(core == 0)
    def _():
        for d in range(1, NY):
            first_y(d).wait_send()
        for q in range(4):
            for copy in first_x[q]:
                copy().wait_send()
            first_pair[q]().wait_send()

    end_down(0)
    end_down(1)
    for col in range(2):

        @pl.when(c == col)
        def _():
            @pl.loop(1, 32)
            def _(d):
                share_copy(col, lax.rem(c + d, 32)).wait_send()

    @pl.when(z == 0)
    def _():
        @pl.loop(1, NZ)
        def _(d):
            rhs_copy(d).wait_send()
            slab_copy(d).wait_send()


def move(cov, obs):
    any_space = pl.BlockSpec(memory_space=pl.ANY)
    vmem = pl.BlockSpec(memory_space=pltpu.VMEM)
    return pl.pallas_call(
        move_kernel,
        out_shape=[
            jax.ShapeDtypeStruct((2, NY, NX, 16, 1024), jnp.float32),
            jax.ShapeDtypeStruct((2, NY, NX, 16, 256), jnp.float32),
            jax.ShapeDtypeStruct((2, NZ, 64, 512), jnp.float32),
            jax.ShapeDtypeStruct((1024, 1024), jnp.float32),
            jax.ShapeDtypeStruct((8, 128, 128), jnp.float32),
        ],
        in_specs=[any_space] * 2,
        out_specs=[any_space] * 3 + [vmem] * 2,
        scratch_shapes=[
            pltpu.VMEM((2, NY, NX, 16, 1024), jnp.float32),
            pltpu.VMEM((512, 512), jnp.float32),
            pltpu.VMEM((128, 128), jnp.float32),
            pltpu.VMEM((128, 128), jnp.float32),
            pltpu.SemaphoreType.DMA((96,)),
            pltpu.SemaphoreType.DMA((96,)),
            pltpu.SemaphoreType.DMA((15,)),
            pltpu.SemaphoreType.DMA((5,)),
        ],
        compiler_params=pltpu.CompilerParams(
            collective_id=0, has_side_effects=True, vmem_limit_bytes=60 * 1024 * 1024
        ),
    )(cov, obs)


def update_kernel(
    upper_ref, inverses_ref, rhs_ref, cross_ref, panel_ref, cov_ref, obs_ref, out_ref, red_ref,
    u, inv, g, x, tile, flat, inv2, sems,
):
    p = lax.axis_index("prow")
    c = lax.axis_index("pcol")
    loads = [
        pltpu.make_async_copy(inverses_ref, inv, sems.at[0]),
        pltpu.make_async_copy(upper_ref, u, sems.at[1]),
        pltpu.make_async_copy(rhs_ref, g.at[:, 512:768], sems.at[2]),
        pltpu.make_async_copy(cross_ref, g.at[:, 0:512], sems.at[3]),
        pltpu.make_async_copy(panel_ref, x, sems.at[4]),
        pltpu.make_async_copy(cov_ref, tile, sems.at[5]),
    ]
    for load in loads:
        load.start()
    for load in loads[:2]:
        load.wait()
    for big in range(4):
        lo, mid, hi = 256 * big, 256 * big + 128, 256 * big + 256
        ia, ib = inv[2 * big], inv[2 * big + 1]
        inv2[big, 0:128, 0:128] = ia
        inv2[big, 0:128, 128:256] = jnp.zeros((128, 128), jnp.float32)
        inv2[big, 128:256, 0:128] = -nn(ib, tn(u[lo:mid, mid:hi], ia, HIGHEST), HIGHEST)
        inv2[big, 128:256, 128:256] = ib
    for load in loads[2:5]:
        load.wait()
    for big in range(4):
        lo, hi = 256 * big, 256 * big + 256
        g[lo:hi, :] = nn(inv2[big], g[lo:hi, :])
        for row in range(hi, 1024, 256):
            g[row : row + 256, :] -= tn(u[lo:hi, row : row + 256], g[lo:hi, :])

        @pl.loop(0, 4)
        def _(i):
            at = pl.ds(pl.multiple_of(i * 256, 256), 256)
            solved = nt(x[at, lo:hi], inv2[big])
            x[at, lo:hi] = solved
            for start in range(hi, 1024, 256):
                x[at, start : start + 256] -= nn(solved, u[lo:hi, start : start + 256])

    loads[5].wait()
    sub = lax.broadcasted_iota(jnp.int32, (256, 512), 0)
    lane = lax.broadcasted_iota(jnp.int32, (256, 512), 1)

    def put(i, values):
        for row in range(32):
            for col in range(4):
                flat[pl.ds(1024 * i + 32 * row + col, 8, stride=4), :] = values[
                    8 * row : 8 * row + 8, 128 * col : 128 * col + 128
                ]

    for i in range(4):
        at = pl.ds(256 * i, 256)
        below = p + 16 * (i // 2)

        @pl.when(c <= 1)
        def _():
            half = jnp.where(c == 0, x[at, 0:512], x[at, 512:1024])
            row = sub + 256 * (i % 2)
            keep = (below > c) | ((below == c) & (row >= lane))
            put(i, jnp.where(keep, half, 0.0))

        @pl.when((c > 1) & (below >= c))
        def _():
            put(i, tile[at, :] - nn(x[at, :], g[:, 0:512]))

        @pl.when((c > 1) & (below < c))
        def _():
            flat[pl.ds(1024 * i, 1024), :] = jnp.zeros((1024, 128), jnp.float32)

    tile_out = pltpu.make_async_copy(flat, out_ref, sems.at[6])
    tile_out.start()
    solved_rhs = g[:, 512:768]
    low = x[pl.ds(pl.multiple_of(16 * c, 16), 16), :]
    high = x[pl.ds(pl.multiple_of(512 + 16 * c, 16), 16), :]
    red_ref[1] = obs_ref[1] - nn(high, solved_rhs)

    @pl.when(p > 1)
    def _():
        red_ref[0] = obs_ref[0] - nn(low, solved_rhs)

    @pl.when(p <= 1)
    def _():
        red_ref[0] = g[pl.ds(pl.multiple_of(512 * p + 16 * c, 16), 16), 512:768]

    tile_out.wait()


def update(upper, inverses, rhs, cross, panel, cov, obs):
    any_space = pl.BlockSpec(memory_space=pl.ANY)
    vmem = pl.BlockSpec(memory_space=pltpu.VMEM)
    return pl.pallas_call(
        update_kernel,
        out_shape=[
            jax.ShapeDtypeStruct((4096, 128), jnp.float32),
            jax.ShapeDtypeStruct((2, 16, 256), jnp.float32),
        ],
        in_specs=[any_space] * 6 + [vmem],
        out_specs=[any_space, vmem],
        scratch_shapes=[
            pltpu.VMEM((1024, 1024), jnp.float32),
            pltpu.VMEM((8, 128, 128), jnp.float32),
            pltpu.VMEM((1024, 768), jnp.float32),
            pltpu.VMEM((1024, 1024), jnp.float32),
            pltpu.VMEM((1024, 512), jnp.float32),
            pltpu.VMEM((4096, 128), jnp.float32),
            pltpu.VMEM((4, 256, 256), jnp.float32),
            pltpu.SemaphoreType.DMA((7,)),
        ],
        compiler_params=pltpu.CompilerParams(vmem_limit_bytes=60 * 1024 * 1024),
    )(upper, inverses, rhs, cross, panel, cov, obs)


def body(covariance, observations):
    cov = covariance.reshape(2, 512, 512)
    obs = observations.reshape(2, 16, 256)
    panel, rhs, cross, upper, inverses = move(cov, obs)
    factor, reduced = update(
        upper, inverses, rhs.reshape(1024, 256), cross.reshape(1024, 512),
        panel.reshape(1024, 1024), cov.reshape(1024, 512), obs,
    )
    return factor.reshape(covariance.shape), reduced.reshape(observations.shape)


def solution(mesh):
    return jax.shard_map(
        body,
        mesh=mesh,
        in_specs=(P(None, "prow", None, None, "pcol", None), P(None, "prow", "pcol", None)),
        out_specs=(P(None, "prow", None, None, "pcol", None), P(None, "prow", "pcol", None)),
        check_vma=False,
    )
```

```python
import functools

import jax
import jax.numpy as jnp
from jax import lax
from jax.experimental import pallas as pl
from jax.experimental.pallas import tpu as pltpu
from jax.sharding import PartitionSpec as P

HIGHEST = lax.Precision.HIGHEST
HIGH = lax.Precision.HIGH
MESH = pl.DeviceIdType.MESH
ROWS8 = 8
NY, NX, NZ = 8, 4, 8


def tn(a, b, precision=HIGH):
    return lax.dot_general(
        a, b, (((0,), (0,)), ((), ())), precision=precision, preferred_element_type=jnp.float32
    )


def nt(a, b, precision=HIGH):
    return lax.dot_general(
        a, b, (((1,), (1,)), ((), ())), precision=precision, preferred_element_type=jnp.float32
    )


def nn(a, b, precision=HIGH):
    return lax.dot_general(
        a, b, (((1,), (0,)), ((), ())), precision=precision, preferred_element_type=jnp.float32
    )


def lane_copy(x, i):
    return jnp.broadcast_to(x[:, i : i + 1], (8, 128))


def row_copy(ref, row):
    return ref[pl.ds(row, 8, stride=0), :]


def factor128(block, inv_ref, row_ref, col_ref, window=2, ahead=2, precision=HIGHEST):
    sub = lax.broadcasted_iota(jnp.int32, (8, 128), 0)
    lane = lax.broadcasted_iota(jnp.int32, (8, 128), 1)
    count = 16
    tiles = [block[8 * i : 8 * i + 8, :] for i in range(count)]
    group = []
    for t in range(count):
        g = t // window
        here = (lane >= 8 * t) & (lane < 8 * t + 8)
        row_ref[8 * t : 8 * t + 8, :] = tiles[t]
        rows = [
            jnp.where(here, jnp.where(lane == 8 * t + i, 1.0, 0.0), row_copy(row_ref, 8 * t + i))
            for i in range(8)
        ]
        base = 64 * (t % 2)
        for j in range(8):
            col_ref[base + 8 * j : base + 8 * j + 8, :] = lane_copy(tiles[t], 8 * t + j)
        s = {(i, k): row_copy(col_ref, base + 8 * i + k) for i in range(8) for k in range(i, 8)}
        later = list(range(t + 1, min((g + 1) * window + ahead, count)))
        cols = {q: [lane_copy(tiles[q], 8 * t + j) for j in range(8)] for q in later}
        rest = {q: jnp.where(here, 0.0, tiles[q]) for q in later}
        for j in range(8):
            r = lax.rsqrt(s[j, j])
            u = {k: s[j, k] * r for k in range(j + 1, 8)}
            for i in range(j + 1, 8):
                for k in range(i, 8):
                    s[i, k] = s[i, k] - u[i] * u[k]
            rows[j] = rows[j] * r
            for i in range(j + 1, 8):
                rows[i] = rows[i] - u[i] * rows[j]
            for q in later:
                m = cols[q][j] * r
                for k in range(j + 1, 8):
                    cols[q][k] = cols[q][k] - m * u[k]
                rest[q] = rest[q] - m * rows[j]
        done = rows[0]
        for i in range(1, 8):
            done = jnp.where(sub == i, rows[i], done)
        inv_ref[8 * t : 8 * t + 8, :] = jnp.where(lane < 8 * t + 8, done, 0.0)
        group.append(done)
        for q in later:
            tiles[q] = rest[q]
        if t % window == window - 1:
            first = (g + 1) * window + ahead
            if first < count:
                inside = (lane >= 8 * g * window) & (lane < 8 * (g + 1) * window)
                right = [
                    jnp.where(
                        (lane >= 8 * (g * window + a + 1)) & (lane < 8 * (g + 1) * window),
                        0.0,
                        group[a],
                    )
                    for a in range(window)
                ]
                v = tn(jnp.concatenate(group, 0), jnp.concatenate(right, 0), precision)
                for i in range(first, count):
                    tiles[i] = jnp.where(inside, 0.0, tiles[i]) - v[8 * i : 8 * i + 8, :]
            group = []


class Mover:
    def __init__(self, send_sems, recv_sems):
        self.send_sems, self.recv_sems, self.used, self.sent = send_sems, recv_sems, 0, []

    def copy(self, src, dst, device):
        slot = self.used
        self.used += 1

        def build():
            return pltpu.make_async_remote_copy(
                src_ref=src(), dst_ref=dst(), send_sem=self.send_sems.at[slot],
                recv_sem=self.recv_sems.at[slot], device_id=device, device_id_type=MESH,
            )

        return build


def all_to_all_peers(mover, views, size, me, device, active=None):
    copies = [
        mover.copy(functools.partial(view, me), functools.partial(view, me), device(lax.rem(me + d, size)))
        for view in views
        for d in range(1, size)
    ]

    def start():
        for copy in copies:
            copy().start()

    def wait():
        for copy in copies:
            copy().wait_recv()

    def end():
        for copy in copies:
            copy().wait_send()

    def guarded(f):
        if active is None:
            return f
        return lambda: pl.when(active)(f)

    mover.sent.append(guarded(end))
    return guarded(start), guarded(wait)


def ring(mover, view, size, me, device, active=None):
    steps = []
    for hop in range(1, size // 2 + 1):
        copies = []
        for side, step in ((0, 1), (1, -1)):
            part = side if hop == size // 2 else None
            block = lax.rem(me - step * (hop - 1) + 2 * size, size)
            ref = functools.partial(view, block, part)
            copies.append(mover.copy(ref, ref, device(lax.rem(me + step + size, size))))

        def start(copies=copies):
            for copy in copies:
                copy().start()

        def wait(copies=copies):
            for copy in copies:
                copy().wait_recv()

        def end(copies=copies):
            for copy in copies:
                copy().wait_send()

        if active is not None:
            start, wait, end = (
                functools.partial(lambda f: pl.when(active)(f), f) for f in (start, wait, end)
            )
        mover.sent.append(end)
        steps.append((start, wait))
    return steps


def move_kernel(
    cov_ref, obs_ref, panel, rhs, cross, upper, inverses,
    lead, stage, work, row_ref, col_ref, send_sems, recv_sems, wide_sems, local_sems,
):
    p = lax.axis_index("prow")
    c = lax.axis_index("pcol")
    z, core = p // 2, lax.rem(p, 2)
    y, x = c // NX, lax.rem(c, NX)

    def at(zz, yy, xx, cc=core):
        return (2 * zz + cc, yy * NX + xx)

    def x_device(v):
        return at(z, y, v)

    def y_device(v):
        return at(z, v, x)

    def z_device(v):
        return at(v, y, x)

    sibling = at(z, y, x, 1 - core)

    barrier = pltpu.get_barrier_semaphore()

    def greet(device):
        pl.semaphore_signal(barrier, inc=1, device_id=device, device_id_type=MESH)

    for d in range(1, NY):
        greet(y_device(lax.rem(y + d, NY)))
    for d in range(1, NX):
        greet(x_device(lax.rem(x + d, NX)))
    for d in range(1, NZ):
        greet(z_device(lax.rem(z + d, NZ)))
    greet(sibling)
    for col in range(2):

        @pl.when(c == col)
        def _():
            @pl.loop(1, 32)
            def _(d):
                greet((p, lax.rem(c + d, 32)))

        @pl.when(c != col)
        def _():
            greet((p, col))

    others = NY + NX + NZ - 2
    pl.semaphore_wait(
        barrier,
        others + jnp.where(c != 0, 1, 0) + jnp.where(c != 1, 1, 0) + jnp.where(c <= 1, 31, 0),
    )

    mover = Mover(send_sems, recv_sems)

    def remote(src, dst, send, recv, device):
        return pltpu.make_async_remote_copy(
            src_ref=src, dst_ref=dst, send_sem=wide_sems.at[send], recv_sem=wide_sems.at[recv],
            device_id=device, device_id_type=MESH,
        )

    def local(src, dst, slot):
        return pltpu.make_async_copy(src, dst, local_sems.at[slot])

    def rows16(row, to):
        return cov_ref.at[row, to // NX, lax.rem(to, NX)]

    def lead_home(half, to):
        return stage if half else lead.at[core, to // NX, lax.rem(to, NX), :, 0:512]

    def piece(ref, part):
        rows = pl.ds(pl.multiple_of(8 * (part // 4), 8), 8)
        return ref.at[rows, pl.ds(pl.multiple_of(128 * lax.rem(part, 4), 128), 128)]

    def second(part, ys, xs):
        rows = pl.ds(pl.multiple_of(8 * (part // 4), 8), 8)
        lanes = pl.ds(pl.multiple_of(512 + 128 * lax.rem(part, 4), 128), 128)
        return lead.at[core, ys, xs, rows, lanes]

    def lead_share(half, to):
        dst = lead_home(half, to)
        return remote(rows16(0, to), dst, 2 * half, 2 * half + 1, (p, to))

    def lead_sender(half):
        return (c == half) & ((p == 0) if half == 0 else (z == 0))

    def lead_plane(half):
        return (p == 0) if half == 0 else (z == 0)

    def own_lead(half):
        return local(rows16(0, c), lead_home(half, c), half)

    def start_lead(half):
        @pl.when(lead_sender(half))
        def _():
            @pl.loop(1, 32)
            def _(d):
                lead_share(half, lax.rem(c + d, 32)).start()

            own_lead(half).start()

    def end_lead(half):
        @pl.when(lead_sender(half))
        def _():
            @pl.loop(1, 32)
            def _(d):
                lead_share(half, lax.rem(c + d, 32)).wait_send()

    def wait_lead(half):
        @pl.when(lead_plane(half) & (c != half))
        def _():
            lead_share(half, c).wait_recv()

        @pl.when(lead_sender(half))
        def _():
            own_lead(half).wait()

    def lead_down(half, to):
        if half:
            return remote(piece(stage, to), second(to, y, x), 6, 7, z_device(to))
        ref = lead_home(0, c)
        return remote(ref, ref, 4, 5, z_device(to))

    def own_piece():
        return local(stage.at[0:8, 0:128], lead.at[core, y, x, 0:8, 512:640], 6)

    def on_lead(half, condition):
        return (condition & (core == 0)) if half == 0 else condition

    def start_down(half):
        @pl.when(on_lead(half, z == 0))
        def _():
            @pl.loop(1, NZ)
            def _(d):
                lead_down(half, d).start()

            if half:
                own_piece().start()
                own_piece().wait()

    def wait_down(half):
        @pl.when(on_lead(half, z != 0))
        def _():
            lead_down(half, 0).wait_recv()

    def end_down(half):
        @pl.when(on_lead(half, z == 0))
        def _():
            @pl.loop(1, NZ)
            def _(d):
                lead_down(half, d).wait_send()

    def share_copy(col, to):
        dst = panel.at[0, to // NX, lax.rem(to, NX), :, 512 * col : 512 * col + 512]
        return remote(rows16(0, to), dst, 8, 9 + col, (p, to))

    def high_part(col, to):
        return panel.at[1, to, :, :, 512 * col : 512 * col + 512]

    def high_share(col, to):
        return remote(cov_ref.at[1, to], high_part(col, to), 15, 16 + col, y_device(to))

    def high_cast(col, to):
        return remote(high_part(col, y), high_part(col, y), 18, 19 + col, x_device(to))

    def slab_copy(to):
        return remote(cov_ref.at[0, to], cross.at[core, to], 11, 12, z_device(to))

    def rhs_copy(to):
        return remote(obs_ref.at[0], rhs.at[core, y, x], 13, 14, z_device(to))

    def own_high(col):
        return local(cov_ref.at[1, 0], high_part(col, 0), 5)

    def own_low(col):
        return local(rows16(0, c), panel.at[0, y, x, :, 512 * col : 512 * col + 512], 3)

    def own_rhs():
        return local(obs_ref.at[0], rhs.at[core, y, x], 2)

    def own_slab():
        return local(cov_ref.at[0, 0], cross.at[core, 0], 4)

    def both_columns(condition, action):
        for col in range(2):
            pl.when(condition(col))(functools.partial(action, col))

    start_lead(0)
    start_lead(1)

    def start_high(col):
        for d in range(1, NY):
            high_share(col, d).start()
        own_high(col).start()

    both_columns(lambda col: c == col, start_high)

    @pl.when(z == 0)
    def _():
        for d in range(1, NZ):
            rhs_copy(d).start()
        own_rhs().start()

    def start_low(col):
        @pl.loop(1, 32)
        def _(d):
            share_copy(col, lax.rem(c + d, 32)).start()

        own_low(col).start()

    both_columns(lambda col: (c == col) & (z != 0), start_low)

    def lead_y(half):
        return lambda block: lead.at[core, block, x, :, 512 * half : 512 * half + 512]

    def rhs_y(block):
        return rhs.at[core, block, x]

    def rhs_x(block):
        return rhs.at[core, :, block]

    def peers(views, size, me, device, active=None):
        return all_to_all_peers(mover, views, size, me, device, active)

    first_slots = mover.used
    mover.used += NY

    def first_y(d):
        ref = lead_y(0)(y)
        return pltpu.make_async_remote_copy(
            src_ref=ref, dst_ref=ref, send_sem=send_sems.at[first_slots + d],
            recv_sem=recv_sems.at[first_slots + y], device_id=y_device(lax.rem(y + d, NY)),
            device_id_type=MESH,
        )

    def first_y_wait(v):
        ref = lead_y(0)(v)
        return pltpu.make_async_remote_copy(
            src_ref=ref, dst_ref=ref, send_sem=send_sems.at[first_slots],
            recv_sem=recv_sems.at[first_slots + v], device_id=y_device(v), device_id_type=MESH,
        )

    def pair_rows(q, block):
        return lead.at[0, 2 * q : 2 * q + 2, block, :, 0:512]

    first_x = [
        [
            mover.copy(
                functools.partial(pair_rows, q, x), functools.partial(pair_rows, q, x),
                x_device(lax.rem(x + d, NX)),
            )
            for d in range(1, NX)
        ]
        for q in range(4)
    ]
    first_pair = [
        mover.copy(
            functools.partial(pair_rows, q, slice(0, NX)),
            functools.partial(pair_rows, q, slice(0, NX)), sibling,
        )
        for q in range(4)
    ]

    def y_arrived(q):
        @pl.when(core == 0)
        def _():
            for v in (2 * q, 2 * q + 1):

                @pl.when(y != v)
                def _():
                    first_y_wait(v).wait_recv()

            for copy in first_x[q]:
                copy().start()

    def x_arrived(q):
        @pl.when(core == 0)
        def _():
            for copy in first_x[q]:
                copy().wait_recv()
            first_pair[q]().start()

    def pair_arrived(q):
        @pl.when(core == 1)
        def _():
            first_pair[q]().wait_recv()

    def whole_or_half(view):
        return lambda block, part: view(
            slice(0, NY) if part is None else slice(4 * part, 4 * part + 4), block
        )

    second_y = peers([lambda block: second(z, block, x)], NY, y, y_device)
    second_x = peers([lambda block: second(z, slice(0, NY), block)], NX, x, x_device)
    second_z = ring(
        mover,
        lambda block, part: second(
            block, slice(0, NY) if part is None else slice(4 * part, 4 * part + 4), slice(0, NX)
        ),
        NZ, z, z_device,
    )
    rhs_gather = peers([rhs_y], NY, y, y_device)
    rhs_ring = ring(
        mover, whole_or_half(lambda rows, block: rhs.at[core, rows, block]), NX, x, x_device
    )
    cross_z = peers([lambda block: cross.at[core, block]], NZ, z, z_device)
    low_rows = z // 2
    low_copies = [
        mover.copy(
            lambda: panel.at[0, y, x], lambda: panel.at[0, y, x], y_device(lax.rem(y + d, NY))
        )
        for d in range(1, NY)
    ]

    def low_y_start():
        for d, copy in enumerate(low_copies, 1):
            pl.when(lax.rem(y + d, NY) <= low_rows)(lambda copy=copy: copy().start())

    def low_y_end():
        for d, copy in enumerate(low_copies, 1):
            pl.when(lax.rem(y + d, NY) <= low_rows)(lambda copy=copy: copy().wait_send())

    mover.sent.append(low_y_end)

    def low_y_wait():
        @pl.when(y <= low_rows)
        def _():
            for copy in low_copies:
                copy().wait_recv()

    low_x = ring(
        mover,
        lambda block, part: panel.at[
            0, slice(0, NY) if part is None else slice(4 * part, 4 * part + 4), block
        ],
        NX, x, x_device, y <= low_rows,
    )
    high_y = ring(
        mover,
        lambda block, part: panel.at[
            1, block, slice(0, NX) if part is None else slice(2 * part, 2 * part + 2)
        ],
        NY, y, y_device,
    )

    def to_sibling(view):
        build = mover.copy(view, view, sibling)
        mover.sent.append(lambda: build().wait_send())
        return lambda: build().start(), lambda: build().wait_recv()

    second_pair = to_sibling(lambda: lead.at[core, :, :, :, 512:1024])
    rhs_pair = to_sibling(lambda: rhs.at[core])
    cross_pair = to_sibling(lambda: cross.at[core])

    wait_lead(0)
    start_down(0)
    wait_lead(1)
    start_down(1)
    both_columns(lambda col: (c == col) & (z == 0), start_low)

    @pl.when(z == 0)
    def _():
        for d in range(1, NZ):
            slab_copy(d).start()
        own_slab().start()

    def cast_high(col):
        @pl.when(y != 0)
        def _():
            high_share(col, y).wait_recv()

        @pl.when(y == 0)
        def _():
            own_high(col).wait()

        for d in range(1, NX):
            high_cast(col, lax.rem(x + d, NX)).start()

    def high_arrived():
        for col in range(2):

            @pl.when(x != col)
            def _():
                high_cast(col, col).wait_recv()

    def low_arrived(where):
        both_columns(lambda col: (c != col) & where, lambda col: share_copy(col, c).wait_recv())
        both_columns(lambda col: (c == col) & where, lambda col: own_low(col).wait())
        pl.when(where)(low_y_start)

    both_columns(lambda col: x == col, cast_high)
    wait_down(0)

    @pl.when(core == 0)
    def _():
        for d in range(1, NY):
            first_y(d).start()

    wait_down(1)
    second_y[0]()
    low_arrived(z != 0)
    y_arrived(0)
    y_arrived(1)
    second_y[1]()
    second_x[0]()
    y_arrived(2)
    y_arrived(3)
    second_x[1]()
    second_z[0][0]()
    high_arrived()
    high_y[0][0]()
    x_arrived(0)
    x_arrived(1)
    second_z[0][1]()
    second_z[1][0]()

    @pl.when(z != 0)
    def _():
        rhs_copy(0).wait_recv()
        slab_copy(0).wait_recv()

    @pl.when(z == 0)
    def _():
        own_rhs().wait()
        own_slab().wait()

    low_arrived(z == 0)
    rhs_gather[0]()
    pair_arrived(0)

    def slot0():
        x_arrived(2)
        pair_arrived(1)
        second_z[1][1]()
        second_z[2][0]()
        high_y[0][1]()
        high_y[1][0]()
        low_y_wait()
        low_x[0][0]()

    def slot1():
        x_arrived(3)
        pair_arrived(2)
        second_z[2][1]()
        second_z[3][0]()
        rhs_gather[1]()
        rhs_ring[0][0]()
        high_y[1][1]()
        high_y[2][0]()

    def slot2():
        pair_arrived(3)
        second_z[3][1]()
        second_pair[0]()
        cross_z[0]()
        rhs_ring[0][1]()
        rhs_ring[1][0]()
        low_x[0][1]()
        low_x[1][0]()
        high_y[2][1]()
        high_y[3][0]()

    def slot3():
        second_pair[1]()

    def slot4():
        rhs_ring[1][1]()
        rhs_pair[0]()
        high_y[3][1]()
        low_x[1][1]()

    def slot6():
        cross_z[1]()
        cross_pair[0]()

    def slot7():
        rhs_pair[1]()
        cross_pair[1]()

    slots = {0: slot0, 1: slot1, 2: slot2, 3: slot3, 4: slot4, 6: slot6, 7: slot7}

    upper[...] = jnp.zeros((1024, 1024), jnp.float32)

    @pl.loop(0, 8)
    def _(a):
        at_row = pl.ds(pl.multiple_of(128 * lax.rem(a, 4), 128), 128)
        at_wide = pl.ds(pl.multiple_of(512 * (a // 4), 512), 512)
        at_upper = pl.ds(pl.multiple_of(128 * a, 128), 128)

        @pl.when(a < 4)
        def _():
            for i in range(8):
                work[pl.ds(pl.multiple_of(128 * a + 16 * i, 16), 16), :] = lead[
                    0, 2 * a + i // NX, i % NX, :, 0:512
                ]

        @pl.when(a == 4)
        def _():
            for i in range(32):
                upper[16 * i : 16 * i + 16, 512:1024] = lead[0, i // NX, i % NX, :, 512:1024]
                work[16 * i : 16 * i + 16, :] = lead[1, i // NX, i % NX, :, 512:1024]
            for k in range(4):
                rows = slice(128 * k, 128 * k + 128)
                if k:
                    upper[rows, 512:1024] -= tn(
                        upper[0 : 128 * k, rows], upper[0 : 128 * k, 512:1024], HIGHEST
                    )
                upper[rows, 512:1024] = nn(inverses[k], upper[rows, 512:1024], HIGHEST)

            @pl.loop(0, 4)
            def _(i):
                cut = pl.ds(pl.multiple_of(128 * i, 128), 128)
                left = upper[0:512, pl.ds(pl.multiple_of(512 + 128 * i, 128), 128)]
                work[cut, :] -= tn(left, upper[0:512, 512:1024], HIGHEST)

        work[at_row, :] -= tn(upper[at_wide, at_upper], upper[at_wide, at_wide], HIGHEST)
        factor128(work[at_row, at_row], inverses.at[a], row_ref, col_ref)
        upper[at_upper, at_wide] = nn(inverses[a], work[at_row, :], HIGHEST)
        for index, events in slots.items():
            pl.when(a == index)(events)

    for end in mover.sent:
        end()

    @pl.when(core == 0)
    def _():
        for d in range(1, NY):
            first_y(d).wait_send()
        for q in range(4):
            for copy in first_x[q]:
                copy().wait_send()
            first_pair[q]().wait_send()

    end_lead(0)
    end_lead(1)
    end_down(0)
    end_down(1)
    for col in range(2):

        @pl.when(c == col)
        def _():
            @pl.loop(1, 32)
            def _(d):
                share_copy(col, lax.rem(c + d, 32)).wait_send()

            @pl.loop(1, NY)
            def _(d):
                high_share(col, d).wait_send()

        @pl.when(x == col)
        def _():
            for d in range(1, NX):
                high_cast(col, lax.rem(x + d, NX)).wait_send()

    @pl.when(z == 0)
    def _():
        @pl.loop(1, NZ)
        def _(d):
            rhs_copy(d).wait_send()
            slab_copy(d).wait_send()


def move(cov, obs):
    any_space = pl.BlockSpec(memory_space=pl.ANY)
    vmem = pl.BlockSpec(memory_space=pltpu.VMEM)
    return pl.pallas_call(
        move_kernel,
        out_shape=[
            jax.ShapeDtypeStruct((2, NY, NX, 16, 1024), jnp.float32),
            jax.ShapeDtypeStruct((2, NY, NX, 16, 256), jnp.float32),
            jax.ShapeDtypeStruct((2, NZ, 4, 16, 512), jnp.float32),
            jax.ShapeDtypeStruct((1024, 1024), jnp.float32),
            jax.ShapeDtypeStruct((8, 128, 128), jnp.float32),
        ],
        in_specs=[any_space] * 2,
        out_specs=[any_space] * 3 + [vmem] * 2,
        scratch_shapes=[
            pltpu.VMEM((2, NY, NX, 16, 1024), jnp.float32),
            pltpu.VMEM((16, 512), jnp.float32),
            pltpu.VMEM((512, 512), jnp.float32),
            pltpu.VMEM((128, 128), jnp.float32),
            pltpu.VMEM((128, 128), jnp.float32),
            pltpu.SemaphoreType.DMA((96,)),
            pltpu.SemaphoreType.DMA((96,)),
            pltpu.SemaphoreType.DMA((21,)),
            pltpu.SemaphoreType.DMA((7,)),
        ],
        compiler_params=pltpu.CompilerParams(
            collective_id=0, has_side_effects=True, vmem_limit_bytes=60 * 1024 * 1024
        ),
    )(cov, obs)


def update_kernel(
    upper_ref, inverses_ref, rhs_ref, cross_ref, panel_ref, cov_ref, obs_ref, out_ref, red_ref,
    u, inv, g, x, tile, flat, inv2, sems,
):
    p = lax.axis_index("prow")
    c = lax.axis_index("pcol")
    loads = [
        pltpu.make_async_copy(inverses_ref, inv, sems.at[0]),
        pltpu.make_async_copy(upper_ref, u, sems.at[1]),
        pltpu.make_async_copy(rhs_ref, g.at[:, 512:768], sems.at[2]),
        pltpu.make_async_copy(cross_ref, g.at[:, 0:512], sems.at[3]),
        pltpu.make_async_copy(panel_ref, x, sems.at[4]),
        pltpu.make_async_copy(cov_ref, tile, sems.at[5]),
    ]
    for load in loads:
        load.start()
    for load in loads[:2]:
        load.wait()
    for big in range(4):
        lo, mid, hi = 256 * big, 256 * big + 128, 256 * big + 256
        ia, ib = inv[2 * big], inv[2 * big + 1]
        inv2[big, 0:128, 0:128] = ia
        inv2[big, 0:128, 128:256] = jnp.zeros((128, 128), jnp.float32)
        inv2[big, 128:256, 0:128] = -nn(ib, tn(u[lo:mid, mid:hi], ia, HIGHEST), HIGHEST)
        inv2[big, 128:256, 128:256] = ib
    for load in loads[2:5]:
        load.wait()
    for big in range(4):
        lo, hi = 256 * big, 256 * big + 256
        g[lo:hi, :] = nn(inv2[big], g[lo:hi, :])
        for row in range(hi, 1024, 256):
            g[row : row + 256, :] -= tn(u[lo:hi, row : row + 256], g[lo:hi, :])

        @pl.loop(0, 4)
        def _(i):
            at = pl.ds(pl.multiple_of(i * 256, 256), 256)
            solved = nt(x[at, lo:hi], inv2[big])
            x[at, lo:hi] = solved
            for start in range(hi, 1024, 256):
                x[at, start : start + 256] -= nn(solved, u[lo:hi, start : start + 256])

    loads[5].wait()
    sub = lax.broadcasted_iota(jnp.int32, (256, 512), 0)
    lane = lax.broadcasted_iota(jnp.int32, (256, 512), 1)

    def put(i, values):
        for row in range(32):
            for col in range(4):
                flat[pl.ds(1024 * i + 32 * row + col, 8, stride=4), :] = values[
                    8 * row : 8 * row + 8, 128 * col : 128 * col + 128
                ]

    for i in range(4):
        at = pl.ds(256 * i, 256)
        below = p + 16 * (i // 2)

        @pl.when(c <= 1)
        def _():
            half = jnp.where(c == 0, x[at, 0:512], x[at, 512:1024])
            row = sub + 256 * (i % 2)
            keep = (below > c) | ((below == c) & (row >= lane))
            put(i, jnp.where(keep, half, 0.0))

        @pl.when((c > 1) & (below >= c))
        def _():
            put(i, tile[at, :] - nn(x[at, :], g[:, 0:512]))

        @pl.when((c > 1) & (below < c))
        def _():
            flat[pl.ds(1024 * i, 1024), :] = jnp.zeros((1024, 128), jnp.float32)

    tile_out = pltpu.make_async_copy(flat, out_ref, sems.at[6])
    tile_out.start()
    solved_rhs = g[:, 512:768]
    low = x[pl.ds(pl.multiple_of(16 * c, 16), 16), :]
    high = x[pl.ds(pl.multiple_of(512 + 16 * c, 16), 16), :]
    red_ref[1] = obs_ref[1] - nn(high, solved_rhs)

    @pl.when(p > 1)
    def _():
        red_ref[0] = obs_ref[0] - nn(low, solved_rhs)

    @pl.when(p <= 1)
    def _():
        red_ref[0] = g[pl.ds(pl.multiple_of(512 * p + 16 * c, 16), 16), 512:768]

    tile_out.wait()


def update(upper, inverses, rhs, cross, panel, cov, obs):
    any_space = pl.BlockSpec(memory_space=pl.ANY)
    vmem = pl.BlockSpec(memory_space=pltpu.VMEM)
    return pl.pallas_call(
        update_kernel,
        out_shape=[
            jax.ShapeDtypeStruct((4096, 128), jnp.float32),
            jax.ShapeDtypeStruct((2, 16, 256), jnp.float32),
        ],
        in_specs=[any_space] * 6 + [vmem],
        out_specs=[any_space, vmem],
        scratch_shapes=[
            pltpu.VMEM((1024, 1024), jnp.float32),
            pltpu.VMEM((8, 128, 128), jnp.float32),
            pltpu.VMEM((1024, 768), jnp.float32),
            pltpu.VMEM((1024, 1024), jnp.float32),
            pltpu.VMEM((1024, 512), jnp.float32),
            pltpu.VMEM((4096, 128), jnp.float32),
            pltpu.VMEM((4, 256, 256), jnp.float32),
            pltpu.SemaphoreType.DMA((7,)),
        ],
        compiler_params=pltpu.CompilerParams(vmem_limit_bytes=60 * 1024 * 1024),
    )(upper, inverses, rhs, cross, panel, cov, obs)


def body(covariance, observations):
    cov = covariance.reshape(2, 512, 512)
    obs = observations.reshape(2, 16, 256)
    panel, rhs, cross, upper, inverses = move(cov.reshape(2, NY, NX, 16, 512), obs)
    factor, reduced = update(
        upper, inverses, rhs.reshape(1024, 256), cross.reshape(1024, 512),
        panel.reshape(1024, 1024), cov.reshape(1024, 512), obs,
    )
    return factor.reshape(covariance.shape), reduced.reshape(observations.shape)


def solution(mesh):
    return jax.shard_map(
        body,
        mesh=mesh,
        in_specs=(P(None, "prow", None, None, "pcol", None), P(None, "prow", "pcol", None)),
        out_specs=(P(None, "prow", None, None, "pcol", None), P(None, "prow", "pcol", None)),
        check_vma=False,
    )
```

```python
import functools

import jax
import jax.numpy as jnp
from jax import lax
from jax.experimental import pallas as pl
from jax.experimental.pallas import tpu as pltpu
from jax.sharding import PartitionSpec as P

HIGHEST = lax.Precision.HIGHEST
HIGH = lax.Precision.HIGH
MESH = pl.DeviceIdType.MESH
ROWS8 = 8
NY, NX, NZ = 8, 4, 8


def tn(a, b, precision=HIGH):
    return lax.dot_general(
        a, b, (((0,), (0,)), ((), ())), precision=precision, preferred_element_type=jnp.float32
    )


def nt(a, b, precision=HIGH):
    return lax.dot_general(
        a, b, (((1,), (1,)), ((), ())), precision=precision, preferred_element_type=jnp.float32
    )


def nn(a, b, precision=HIGH):
    return lax.dot_general(
        a, b, (((1,), (0,)), ((), ())), precision=precision, preferred_element_type=jnp.float32
    )


def lane_copy(x, i):
    return jnp.broadcast_to(x[:, i : i + 1], (8, 128))


def row_copy(ref, row):
    return ref[pl.ds(row, 8, stride=0), :]


def factor128(block, inv_ref, row_ref, col_ref, window=2, ahead=2, precision=HIGHEST):
    sub = lax.broadcasted_iota(jnp.int32, (8, 128), 0)
    lane = lax.broadcasted_iota(jnp.int32, (8, 128), 1)
    count = 16
    tiles = [block[8 * i : 8 * i + 8, :] for i in range(count)]
    group = []
    for t in range(count):
        g = t // window
        here = (lane >= 8 * t) & (lane < 8 * t + 8)
        row_ref[8 * t : 8 * t + 8, :] = tiles[t]
        rows = [
            jnp.where(here, jnp.where(lane == 8 * t + i, 1.0, 0.0), row_copy(row_ref, 8 * t + i))
            for i in range(8)
        ]
        base = 64 * (t % 2)
        for j in range(8):
            col_ref[base + 8 * j : base + 8 * j + 8, :] = lane_copy(tiles[t], 8 * t + j)
        s = {(i, k): row_copy(col_ref, base + 8 * i + k) for i in range(8) for k in range(i, 8)}
        later = list(range(t + 1, min((g + 1) * window + ahead, count)))
        cols = {q: [lane_copy(tiles[q], 8 * t + j) for j in range(8)] for q in later}
        rest = {q: jnp.where(here, 0.0, tiles[q]) for q in later}
        for j in range(8):
            r = lax.rsqrt(s[j, j])
            u = {k: s[j, k] * r for k in range(j + 1, 8)}
            for i in range(j + 1, 8):
                for k in range(i, 8):
                    s[i, k] = s[i, k] - u[i] * u[k]
            rows[j] = rows[j] * r
            for i in range(j + 1, 8):
                rows[i] = rows[i] - u[i] * rows[j]
            for q in later:
                m = cols[q][j] * r
                for k in range(j + 1, 8):
                    cols[q][k] = cols[q][k] - m * u[k]
                rest[q] = rest[q] - m * rows[j]
        done = rows[0]
        for i in range(1, 8):
            done = jnp.where(sub == i, rows[i], done)
        inv_ref[8 * t : 8 * t + 8, :] = jnp.where(lane < 8 * t + 8, done, 0.0)
        group.append(done)
        for q in later:
            tiles[q] = rest[q]
        if t % window == window - 1:
            first = (g + 1) * window + ahead
            if first < count:
                inside = (lane >= 8 * g * window) & (lane < 8 * (g + 1) * window)
                right = [
                    jnp.where(
                        (lane >= 8 * (g * window + a + 1)) & (lane < 8 * (g + 1) * window),
                        0.0,
                        group[a],
                    )
                    for a in range(window)
                ]
                v = tn(jnp.concatenate(group, 0), jnp.concatenate(right, 0), precision)
                for i in range(first, count):
                    tiles[i] = jnp.where(inside, 0.0, tiles[i]) - v[8 * i : 8 * i + 8, :]
            group = []


class Mover:
    def __init__(self, send_sems, recv_sems):
        self.send_sems, self.recv_sems, self.used, self.sent = send_sems, recv_sems, 0, []

    def copy(self, src, dst, device):
        slot = self.used
        self.used += 1

        def build():
            return pltpu.make_async_remote_copy(
                src_ref=src(), dst_ref=dst(), send_sem=self.send_sems.at[slot],
                recv_sem=self.recv_sems.at[slot], device_id=device, device_id_type=MESH,
            )

        return build


def all_to_all_peers(mover, views, size, me, device, active=None):
    copies = [
        mover.copy(functools.partial(view, me), functools.partial(view, me), device(lax.rem(me + d, size)))
        for view in views
        for d in range(1, size)
    ]

    def start():
        for copy in copies:
            copy().start()

    def wait():
        for copy in copies:
            copy().wait_recv()

    def end():
        for copy in copies:
            copy().wait_send()

    def guarded(f):
        if active is None:
            return f
        return lambda: pl.when(active)(f)

    mover.sent.append(guarded(end))
    return guarded(start), guarded(wait)


def ring(mover, view, size, me, device, active=None):
    steps = []
    for hop in range(1, size // 2 + 1):
        copies = []
        for side, step in ((0, 1), (1, -1)):
            part = side if hop == size // 2 else None
            block = lax.rem(me - step * (hop - 1) + 2 * size, size)
            ref = functools.partial(view, block, part)
            copies.append(mover.copy(ref, ref, device(lax.rem(me + step + size, size))))

        def start(copies=copies):
            for copy in copies:
                copy().start()

        def wait(copies=copies):
            for copy in copies:
                copy().wait_recv()

        def end(copies=copies):
            for copy in copies:
                copy().wait_send()

        if active is not None:
            start, wait, end = (
                functools.partial(lambda f: pl.when(active)(f), f) for f in (start, wait, end)
            )
        mover.sent.append(end)
        steps.append((start, wait))
    return steps


def move_kernel(
    cov_ref, obs_ref, panel, rhs, cross, upper, inverses,
    lead, stage, work, row_ref, col_ref, send_sems, recv_sems, wide_sems, local_sems,
):
    p = lax.axis_index("prow")
    c = lax.axis_index("pcol")
    z, core = p // 2, lax.rem(p, 2)
    y, x = c // NX, lax.rem(c, NX)

    def at(zz, yy, xx, cc=core):
        return (2 * zz + cc, yy * NX + xx)

    def x_device(v):
        return at(z, y, v)

    def y_device(v):
        return at(z, v, x)

    def z_device(v):
        return at(v, y, x)

    sibling = at(z, y, x, 1 - core)

    barrier = pltpu.get_barrier_semaphore()

    def greet(device):
        pl.semaphore_signal(barrier, inc=1, device_id=device, device_id_type=MESH)

    for d in range(1, NY):
        greet(y_device(lax.rem(y + d, NY)))
    for d in range(1, NX):
        greet(x_device(lax.rem(x + d, NX)))
    for d in range(1, NZ):
        greet(z_device(lax.rem(z + d, NZ)))
    greet(sibling)
    for col in range(2):

        @pl.when(c == col)
        def _():
            @pl.loop(1, 32)
            def _(d):
                greet((p, lax.rem(c + d, 32)))

        @pl.when(c != col)
        def _():
            greet((p, col))

    others = NY + NX + NZ - 2
    pl.semaphore_wait(
        barrier,
        others + jnp.where(c != 0, 1, 0) + jnp.where(c != 1, 1, 0) + jnp.where(c <= 1, 31, 0),
    )

    mover = Mover(send_sems, recv_sems)

    def remote(src, dst, send, recv, device):
        return pltpu.make_async_remote_copy(
            src_ref=src, dst_ref=dst, send_sem=wide_sems.at[send], recv_sem=wide_sems.at[recv],
            device_id=device, device_id_type=MESH,
        )

    def local(src, dst, slot):
        return pltpu.make_async_copy(src, dst, local_sems.at[slot])

    def rows16(row, to):
        return cov_ref.at[row, to // NX, lax.rem(to, NX)]

    def lead_home(half, to):
        return stage if half else lead.at[core, to // NX, lax.rem(to, NX), :, 0:512]

    def piece(ref, part):
        rows = pl.ds(pl.multiple_of(8 * (part // 4), 8), 8)
        return ref.at[rows, pl.ds(pl.multiple_of(128 * lax.rem(part, 4), 128), 128)]

    def second(part, ys, xs):
        rows = pl.ds(pl.multiple_of(8 * (part // 4), 8), 8)
        lanes = pl.ds(pl.multiple_of(512 + 128 * lax.rem(part, 4), 128), 128)
        return lead.at[core, ys, xs, rows, lanes]

    def lead_share(half, to):
        dst = lead_home(half, to)
        return remote(rows16(0, to), dst, 2 * half, 2 * half + 1, (p, to))

    def lead_sender(half):
        return (c == half) & ((p == 0) if half == 0 else (z == 0))

    def lead_plane(half):
        return (p == 0) if half == 0 else (z == 0)

    def own_lead(half):
        return local(rows16(0, c), lead_home(half, c), half)

    def start_lead(half):
        @pl.when(lead_sender(half))
        def _():
            @pl.loop(1, 32)
            def _(d):
                lead_share(half, lax.rem(c + d, 32)).start()

            own_lead(half).start()

    def end_lead(half):
        @pl.when(lead_sender(half))
        def _():
            @pl.loop(1, 32)
            def _(d):
                lead_share(half, lax.rem(c + d, 32)).wait_send()

    def wait_lead(half):
        @pl.when(lead_plane(half) & (c != half))
        def _():
            lead_share(half, c).wait_recv()

        @pl.when(lead_sender(half))
        def _():
            own_lead(half).wait()

    def lead_down(half, to):
        if half:
            return remote(piece(stage, to), second(to, y, x), 6, 7, z_device(to))
        ref = lead_home(0, c)
        return remote(ref, ref, 4, 5, z_device(to))

    def own_piece():
        return local(stage.at[0:8, 0:128], lead.at[core, y, x, 0:8, 512:640], 6)

    def on_lead(half, condition):
        return (condition & (core == 0)) if half == 0 else condition

    def start_down(half):
        @pl.when(on_lead(half, z == 0))
        def _():
            @pl.loop(1, NZ)
            def _(d):
                lead_down(half, d).start()

            if half:
                own_piece().start()
                own_piece().wait()

    def wait_down(half):
        @pl.when(on_lead(half, z != 0))
        def _():
            lead_down(half, 0).wait_recv()

    def end_down(half):
        @pl.when(on_lead(half, z == 0))
        def _():
            @pl.loop(1, NZ)
            def _(d):
                lead_down(half, d).wait_send()

    def share_copy(col, to):
        dst = panel.at[0, to // NX, lax.rem(to, NX), :, 512 * col : 512 * col + 512]
        return remote(rows16(0, to), dst, 8, 9 + col, (p, to))

    def high_part(col, to):
        return panel.at[1, to, :, :, 512 * col : 512 * col + 512]

    def high_share(col, to):
        return remote(cov_ref.at[1, to], high_part(col, to), 15, 16 + col, y_device(to))

    def high_cast(col, to):
        return remote(high_part(col, y), high_part(col, y), 18, 19 + col, x_device(to))

    def slab_copy(to):
        return remote(cov_ref.at[0, to], cross.at[core, to], 11, 12, z_device(to))

    def rhs_copy(to):
        return remote(obs_ref.at[0], rhs.at[core, y, x], 13, 14, z_device(to))

    def own_high(col):
        return local(cov_ref.at[1, 0], high_part(col, 0), 5)

    def own_low(col):
        return local(rows16(0, c), panel.at[0, y, x, :, 512 * col : 512 * col + 512], 3)

    def own_rhs():
        return local(obs_ref.at[0], rhs.at[core, y, x], 2)

    def own_slab():
        return local(cov_ref.at[0, 0], cross.at[core, 0], 4)

    def both_columns(condition, action):
        for col in range(2):
            pl.when(condition(col))(functools.partial(action, col))

    start_lead(0)
    start_lead(1)

    def start_high(col):
        for d in range(1, NY):
            high_share(col, d).start()
        own_high(col).start()

    both_columns(lambda col: c == col, start_high)

    @pl.when(z == 0)
    def _():
        for d in range(1, NZ):
            rhs_copy(d).start()
        own_rhs().start()

    def start_low(col):
        @pl.loop(1, 32)
        def _(d):
            share_copy(col, lax.rem(c + d, 32)).start()

        own_low(col).start()

    def lead_y(half):
        return lambda block: lead.at[core, block, x, :, 512 * half : 512 * half + 512]

    def rhs_y(block):
        return rhs.at[core, block, x]

    def rhs_x(block):
        return rhs.at[core, :, block]

    def peers(views, size, me, device, active=None):
        return all_to_all_peers(mover, views, size, me, device, active)

    first_slots = mover.used
    mover.used += NY

    def first_y(d):
        ref = lead_y(0)(y)
        return pltpu.make_async_remote_copy(
            src_ref=ref, dst_ref=ref, send_sem=send_sems.at[first_slots + d],
            recv_sem=recv_sems.at[first_slots + y], device_id=y_device(lax.rem(y + d, NY)),
            device_id_type=MESH,
        )

    def first_y_wait(v):
        ref = lead_y(0)(v)
        return pltpu.make_async_remote_copy(
            src_ref=ref, dst_ref=ref, send_sem=send_sems.at[first_slots],
            recv_sem=recv_sems.at[first_slots + v], device_id=y_device(v), device_id_type=MESH,
        )

    def pair_rows(q, block):
        return lead.at[0, 2 * q : 2 * q + 2, block, :, 0:512]

    first_x = [
        [
            mover.copy(
                functools.partial(pair_rows, q, x), functools.partial(pair_rows, q, x),
                x_device(lax.rem(x + d, NX)),
            )
            for d in range(1, NX)
        ]
        for q in range(4)
    ]
    first_pair = [
        mover.copy(
            functools.partial(pair_rows, q, slice(0, NX)),
            functools.partial(pair_rows, q, slice(0, NX)), sibling,
        )
        for q in range(4)
    ]

    def y_arrived(q):
        @pl.when(core == 0)
        def _():
            for v in (2 * q, 2 * q + 1):

                @pl.when(y != v)
                def _():
                    first_y_wait(v).wait_recv()

            for copy in first_x[q]:
                copy().start()

    def x_arrived(q):
        @pl.when(core == 0)
        def _():
            for copy in first_x[q]:
                copy().wait_recv()
            first_pair[q]().start()

    def pair_arrived(q):
        @pl.when(core == 1)
        def _():
            first_pair[q]().wait_recv()

    def whole_or_half(view):
        return lambda block, part: view(
            slice(0, NY) if part is None else slice(4 * part, 4 * part + 4), block
        )

    second_y = peers([lambda block: second(z, block, x)], NY, y, y_device)
    second_x = peers([lambda block: second(z, slice(0, NY), block)], NX, x, x_device)
    second_z = ring(
        mover,
        lambda block, part: second(
            block, slice(0, NY) if part is None else slice(4 * part, 4 * part + 4), slice(0, NX)
        ),
        NZ, z, z_device,
    )
    rhs_gather = peers([rhs_y], NY, y, y_device)
    rhs_ring = ring(
        mover, whole_or_half(lambda rows, block: rhs.at[core, rows, block]), NX, x, x_device
    )
    cross_z = ring(
        mover,
        lambda block, part: (
            cross.at[core, block] if part is None else cross.at[core, block, 2 * part : 2 * part + 2]
        ),
        NZ, z, z_device,
    )
    low_rows = z // 2
    low_copies = [
        mover.copy(
            lambda: panel.at[0, y, x], lambda: panel.at[0, y, x], y_device(lax.rem(y + d, NY))
        )
        for d in range(1, NY)
    ]

    def low_y_start():
        for d, copy in enumerate(low_copies, 1):
            pl.when(lax.rem(y + d, NY) <= low_rows)(lambda copy=copy: copy().start())

    def low_y_end():
        for d, copy in enumerate(low_copies, 1):
            pl.when(lax.rem(y + d, NY) <= low_rows)(lambda copy=copy: copy().wait_send())

    mover.sent.append(low_y_end)

    def low_y_wait():
        @pl.when(y <= low_rows)
        def _():
            for copy in low_copies:
                copy().wait_recv()

    low_x = ring(
        mover,
        lambda block, part: panel.at[
            0, slice(0, NY) if part is None else slice(4 * part, 4 * part + 4), block
        ],
        NX, x, x_device, y <= low_rows,
    )
    high_y = ring(
        mover,
        lambda block, part: panel.at[
            1, block, slice(0, NX) if part is None else slice(2 * part, 2 * part + 2)
        ],
        NY, y, y_device,
    )

    def to_sibling(view):
        build = mover.copy(view, view, sibling)
        mover.sent.append(lambda: build().wait_send())
        return lambda: build().start(), lambda: build().wait_recv()

    second_pair = to_sibling(lambda: lead.at[core, :, :, :, 512:1024])
    rhs_pair = to_sibling(lambda: rhs.at[core])
    cross_pair = to_sibling(lambda: cross.at[core])

    wait_lead(0)
    start_down(0)
    wait_lead(1)
    start_down(1)
    @pl.when(z == 0)
    def _():
        for d in range(1, NZ):
            slab_copy(d).start()
        own_slab().start()

    def cast_high(col):
        @pl.when(y != 0)
        def _():
            high_share(col, y).wait_recv()

        @pl.when(y == 0)
        def _():
            own_high(col).wait()

        for d in range(1, NX):
            high_cast(col, lax.rem(x + d, NX)).start()

    def high_arrived():
        for col in range(2):

            @pl.when(x != col)
            def _():
                high_cast(col, col).wait_recv()

    def low_arrived():
        both_columns(lambda col: c != col, lambda col: share_copy(col, c).wait_recv())
        both_columns(lambda col: c == col, lambda col: own_low(col).wait())
        low_y_start()

    wait_down(0)

    @pl.when(core == 0)
    def _():
        for d in range(1, NY):
            first_y(d).start()

    wait_down(1)
    second_y[0]()
    y_arrived(0)
    y_arrived(1)
    second_y[1]()
    second_x[0]()
    y_arrived(2)
    y_arrived(3)
    both_columns(lambda col: c == col, start_low)
    second_x[1]()
    second_z[0][0]()
    x_arrived(0)
    x_arrived(1)
    both_columns(lambda col: x == col, cast_high)
    second_z[0][1]()
    second_z[1][0]()

    @pl.when(z != 0)
    def _():
        rhs_copy(0).wait_recv()
        slab_copy(0).wait_recv()

    @pl.when(z == 0)
    def _():
        own_rhs().wait()
        own_slab().wait()

    cross_z[0][0]()
    rhs_gather[0]()
    pair_arrived(0)

    def slot0():
        x_arrived(2)
        pair_arrived(1)
        second_z[1][1]()
        second_z[2][0]()
        cross_z[0][1]()
        cross_z[1][0]()
        low_arrived()

    def slot1():
        x_arrived(3)
        pair_arrived(2)
        second_z[2][1]()
        second_z[3][0]()
        high_arrived()
        high_y[0][0]()
        cross_z[1][1]()
        cross_z[2][0]()

    def slot2():
        pair_arrived(3)
        second_z[3][1]()
        second_pair[0]()
        high_y[0][1]()
        high_y[1][0]()
        low_y_wait()
        low_x[0][0]()
        cross_z[2][1]()
        cross_z[3][0]()
        rhs_gather[1]()

    def slot3():
        second_pair[1]()
        high_y[1][1]()
        high_y[2][0]()
        cross_z[3][1]()
        cross_pair[0]()
        rhs_ring[0][0]()

    def slot4():
        high_y[2][1]()
        high_y[3][0]()
        low_x[0][1]()
        low_x[1][0]()
        rhs_ring[0][1]()
        rhs_ring[1][0]()

    def slot5():
        rhs_ring[1][1]()
        rhs_pair[0]()

    def slot6():
        high_y[3][1]()
        low_x[1][1]()
        rhs_pair[1]()
        cross_pair[1]()

    slots = {0: slot0, 1: slot1, 2: slot2, 3: slot3, 4: slot4, 5: slot5, 6: slot6}

    upper[...] = jnp.zeros((1024, 1024), jnp.float32)

    @pl.loop(0, 8)
    def _(a):
        at_row = pl.ds(pl.multiple_of(128 * lax.rem(a, 4), 128), 128)
        at_wide = pl.ds(pl.multiple_of(512 * (a // 4), 512), 512)
        at_upper = pl.ds(pl.multiple_of(128 * a, 128), 128)

        @pl.when(a < 4)
        def _():
            for i in range(8):
                work[pl.ds(pl.multiple_of(128 * a + 16 * i, 16), 16), :] = lead[
                    0, 2 * a + i // NX, i % NX, :, 0:512
                ]

        @pl.when(a == 4)
        def _():
            for i in range(32):
                upper[16 * i : 16 * i + 16, 512:1024] = lead[0, i // NX, i % NX, :, 512:1024]
                work[16 * i : 16 * i + 16, :] = lead[1, i // NX, i % NX, :, 512:1024]
            for k in range(4):
                rows = slice(128 * k, 128 * k + 128)
                if k:
                    upper[rows, 512:1024] -= tn(
                        upper[0 : 128 * k, rows], upper[0 : 128 * k, 512:1024], HIGHEST
                    )
                upper[rows, 512:1024] = nn(inverses[k], upper[rows, 512:1024], HIGHEST)

            @pl.loop(0, 4)
            def _(i):
                cut = pl.ds(pl.multiple_of(128 * i, 128), 128)
                left = upper[0:512, pl.ds(pl.multiple_of(512 + 128 * i, 128), 128)]
                work[cut, :] -= tn(left, upper[0:512, 512:1024], HIGHEST)

        work[at_row, :] -= tn(upper[at_wide, at_upper], upper[at_wide, at_wide], HIGHEST)
        factor128(work[at_row, at_row], inverses.at[a], row_ref, col_ref)
        upper[at_upper, at_wide] = nn(inverses[a], work[at_row, :], HIGHEST)
        for index, events in slots.items():
            pl.when(a == index)(events)

    for end in mover.sent:
        end()

    @pl.when(core == 0)
    def _():
        for d in range(1, NY):
            first_y(d).wait_send()
        for q in range(4):
            for copy in first_x[q]:
                copy().wait_send()
            first_pair[q]().wait_send()

    end_lead(0)
    end_lead(1)
    end_down(0)
    end_down(1)
    for col in range(2):

        @pl.when(c == col)
        def _():
            @pl.loop(1, 32)
            def _(d):
                share_copy(col, lax.rem(c + d, 32)).wait_send()

            @pl.loop(1, NY)
            def _(d):
                high_share(col, d).wait_send()

        @pl.when(x == col)
        def _():
            for d in range(1, NX):
                high_cast(col, lax.rem(x + d, NX)).wait_send()

    @pl.when(z == 0)
    def _():
        @pl.loop(1, NZ)
        def _(d):
            rhs_copy(d).wait_send()
            slab_copy(d).wait_send()


def move(cov, obs):
    any_space = pl.BlockSpec(memory_space=pl.ANY)
    vmem = pl.BlockSpec(memory_space=pltpu.VMEM)
    return pl.pallas_call(
        move_kernel,
        out_shape=[
            jax.ShapeDtypeStruct((2, NY, NX, 16, 1024), jnp.float32),
            jax.ShapeDtypeStruct((2, NY, NX, 16, 256), jnp.float32),
            jax.ShapeDtypeStruct((2, NZ, 4, 16, 512), jnp.float32),
            jax.ShapeDtypeStruct((1024, 1024), jnp.float32),
            jax.ShapeDtypeStruct((8, 128, 128), jnp.float32),
        ],
        in_specs=[any_space] * 2,
        out_specs=[any_space] * 3 + [vmem] * 2,
        scratch_shapes=[
            pltpu.VMEM((2, NY, NX, 16, 1024), jnp.float32),
            pltpu.VMEM((16, 512), jnp.float32),
            pltpu.VMEM((512, 512), jnp.float32),
            pltpu.VMEM((128, 128), jnp.float32),
            pltpu.VMEM((128, 128), jnp.float32),
            pltpu.SemaphoreType.DMA((96,)),
            pltpu.SemaphoreType.DMA((96,)),
            pltpu.SemaphoreType.DMA((21,)),
            pltpu.SemaphoreType.DMA((7,)),
        ],
        compiler_params=pltpu.CompilerParams(
            collective_id=0, has_side_effects=True, vmem_limit_bytes=60 * 1024 * 1024
        ),
    )(cov, obs)


def update_kernel(
    upper_ref, inverses_ref, rhs_ref, cross_ref, panel_ref, cov_ref, obs_ref, out_ref, red_ref,
    u, inv, g, x, tile, flat, inv2, sems,
):
    p = lax.axis_index("prow")
    c = lax.axis_index("pcol")
    loads = [
        pltpu.make_async_copy(inverses_ref, inv, sems.at[0]),
        pltpu.make_async_copy(upper_ref, u, sems.at[1]),
        pltpu.make_async_copy(rhs_ref, g.at[:, 512:768], sems.at[2]),
        pltpu.make_async_copy(cross_ref, g.at[:, 0:512], sems.at[3]),
        pltpu.make_async_copy(panel_ref, x, sems.at[4]),
        pltpu.make_async_copy(cov_ref, tile, sems.at[5]),
    ]
    for load in loads:
        load.start()
    for load in loads[:2]:
        load.wait()
    for big in range(4):
        lo, mid, hi = 256 * big, 256 * big + 128, 256 * big + 256
        ia, ib = inv[2 * big], inv[2 * big + 1]
        inv2[big, 0:128, 0:128] = ia
        inv2[big, 0:128, 128:256] = jnp.zeros((128, 128), jnp.float32)
        inv2[big, 128:256, 0:128] = -nn(ib, tn(u[lo:mid, mid:hi], ia, HIGHEST), HIGHEST)
        inv2[big, 128:256, 128:256] = ib
    for load in loads[2:5]:
        load.wait()
    for big in range(4):
        lo, hi = 256 * big, 256 * big + 256
        g[lo:hi, :] = nn(inv2[big], g[lo:hi, :])
        for row in range(hi, 1024, 256):
            g[row : row + 256, :] -= tn(u[lo:hi, row : row + 256], g[lo:hi, :])

        for i in range(4):
            at = slice(256 * i, 256 * i + 256)
            solved = nt(x[at, lo:hi], inv2[big])
            x[at, lo:hi] = solved
            for start in range(hi, 1024, 256):
                x[at, start : start + 256] -= nn(solved, u[lo:hi, start : start + 256])

    loads[5].wait()
    sub = lax.broadcasted_iota(jnp.int32, (256, 512), 0)
    lane = lax.broadcasted_iota(jnp.int32, (256, 512), 1)

    def put(i, values):
        for row in range(32):
            for col in range(4):
                flat[pl.ds(1024 * i + 32 * row + col, 8, stride=4), :] = values[
                    8 * row : 8 * row + 8, 128 * col : 128 * col + 128
                ]

    for i in range(4):
        at = pl.ds(256 * i, 256)
        below = p + 16 * (i // 2)

        @pl.when(c <= 1)
        def _():
            half = jnp.where(c == 0, x[at, 0:512], x[at, 512:1024])
            row = sub + 256 * (i % 2)
            keep = (below > c) | ((below == c) & (row >= lane))
            put(i, jnp.where(keep, half, 0.0))

        @pl.when((c > 1) & (below >= c))
        def _():
            put(i, tile[at, :] - nn(x[at, :], g[:, 0:512]))

        @pl.when((c > 1) & (below < c))
        def _():
            flat[pl.ds(1024 * i, 1024), :] = jnp.zeros((1024, 128), jnp.float32)

    tile_out = pltpu.make_async_copy(flat, out_ref, sems.at[6])
    tile_out.start()
    solved_rhs = g[:, 512:768]
    low = x[pl.ds(pl.multiple_of(16 * c, 16), 16), :]
    high = x[pl.ds(pl.multiple_of(512 + 16 * c, 16), 16), :]
    red_ref[1] = obs_ref[1] - nn(high, solved_rhs)

    @pl.when(p > 1)
    def _():
        red_ref[0] = obs_ref[0] - nn(low, solved_rhs)

    @pl.when(p <= 1)
    def _():
        red_ref[0] = g[pl.ds(pl.multiple_of(512 * p + 16 * c, 16), 16), 512:768]

    tile_out.wait()


def update(upper, inverses, rhs, cross, panel, cov, obs):
    any_space = pl.BlockSpec(memory_space=pl.ANY)
    vmem = pl.BlockSpec(memory_space=pltpu.VMEM)
    return pl.pallas_call(
        update_kernel,
        out_shape=[
            jax.ShapeDtypeStruct((4096, 128), jnp.float32),
            jax.ShapeDtypeStruct((2, 16, 256), jnp.float32),
        ],
        in_specs=[any_space] * 6 + [vmem],
        out_specs=[any_space, vmem],
        scratch_shapes=[
            pltpu.VMEM((1024, 1024), jnp.float32),
            pltpu.VMEM((8, 128, 128), jnp.float32),
            pltpu.VMEM((1024, 768), jnp.float32),
            pltpu.VMEM((1024, 1024), jnp.float32),
            pltpu.VMEM((1024, 512), jnp.float32),
            pltpu.VMEM((4096, 128), jnp.float32),
            pltpu.VMEM((4, 256, 256), jnp.float32),
            pltpu.SemaphoreType.DMA((7,)),
        ],
        compiler_params=pltpu.CompilerParams(vmem_limit_bytes=60 * 1024 * 1024),
    )(upper, inverses, rhs, cross, panel, cov, obs)


def body(covariance, observations):
    cov = covariance.reshape(2, 512, 512)
    obs = observations.reshape(2, 16, 256)
    panel, rhs, cross, upper, inverses = move(cov.reshape(2, NY, NX, 16, 512), obs)
    factor, reduced = update(
        upper, inverses, rhs.reshape(1024, 256), cross.reshape(1024, 512),
        panel.reshape(1024, 1024), cov.reshape(1024, 512), obs,
    )
    return factor.reshape(covariance.shape), reduced.reshape(observations.shape)


def solution(mesh):
    return jax.shard_map(
        body,
        mesh=mesh,
        in_specs=(P(None, "prow", None, None, "pcol", None), P(None, "prow", "pcol", None)),
        out_specs=(P(None, "prow", None, None, "pcol", None), P(None, "prow", "pcol", None)),
        check_vma=False,
    )
```

```python
import functools

import jax
import jax.numpy as jnp
from jax import lax
from jax.experimental import pallas as pl
from jax.experimental.pallas import tpu as pltpu
from jax.sharding import PartitionSpec as P

HIGHEST = lax.Precision.HIGHEST
HIGH = lax.Precision.HIGH
MESH = pl.DeviceIdType.MESH
ROWS8 = 8
NY, NX, NZ = 8, 4, 8


def tn(a, b, precision=HIGH):
    return lax.dot_general(
        a, b, (((0,), (0,)), ((), ())), precision=precision, preferred_element_type=jnp.float32
    )


def nt(a, b, precision=HIGH):
    return lax.dot_general(
        a, b, (((1,), (1,)), ((), ())), precision=precision, preferred_element_type=jnp.float32
    )


def nn(a, b, precision=HIGH):
    return lax.dot_general(
        a, b, (((1,), (0,)), ((), ())), precision=precision, preferred_element_type=jnp.float32
    )


def lane_copy(x, i):
    return jnp.broadcast_to(x[:, i : i + 1], (8, 128))


def row_copy(ref, row):
    return ref[pl.ds(row, 8, stride=0), :]


def factor128(block, inv_ref, row_ref, col_ref, window=2, ahead=2, precision=HIGHEST):
    sub = lax.broadcasted_iota(jnp.int32, (8, 128), 0)
    lane = lax.broadcasted_iota(jnp.int32, (8, 128), 1)
    count = 16
    tiles = [block[8 * i : 8 * i + 8, :] for i in range(count)]
    group = []
    for t in range(count):
        g = t // window
        here = (lane >= 8 * t) & (lane < 8 * t + 8)
        row_ref[8 * t : 8 * t + 8, :] = tiles[t]
        rows = [
            jnp.where(here, jnp.where(lane == 8 * t + i, 1.0, 0.0), row_copy(row_ref, 8 * t + i))
            for i in range(8)
        ]
        base = 64 * (t % 2)
        for j in range(8):
            col_ref[base + 8 * j : base + 8 * j + 8, :] = lane_copy(tiles[t], 8 * t + j)
        s = {(i, k): row_copy(col_ref, base + 8 * i + k) for i in range(8) for k in range(i, 8)}
        later = list(range(t + 1, min((g + 1) * window + ahead, count)))
        cols = {q: [lane_copy(tiles[q], 8 * t + j) for j in range(8)] for q in later}
        rest = {q: jnp.where(here, 0.0, tiles[q]) for q in later}
        for j in range(8):
            r = lax.rsqrt(s[j, j])
            u = {k: s[j, k] * r for k in range(j + 1, 8)}
            for i in range(j + 1, 8):
                for k in range(i, 8):
                    s[i, k] = s[i, k] - u[i] * u[k]
            rows[j] = rows[j] * r
            for i in range(j + 1, 8):
                rows[i] = rows[i] - u[i] * rows[j]
            for q in later:
                m = cols[q][j] * r
                for k in range(j + 1, 8):
                    cols[q][k] = cols[q][k] - m * u[k]
                rest[q] = rest[q] - m * rows[j]
        done = rows[0]
        for i in range(1, 8):
            done = jnp.where(sub == i, rows[i], done)
        inv_ref[8 * t : 8 * t + 8, :] = jnp.where(lane < 8 * t + 8, done, 0.0)
        group.append(done)
        for q in later:
            tiles[q] = rest[q]
        if t % window == window - 1:
            first = (g + 1) * window + ahead
            if first < count:
                inside = (lane >= 8 * g * window) & (lane < 8 * (g + 1) * window)
                right = [
                    jnp.where(
                        (lane >= 8 * (g * window + a + 1)) & (lane < 8 * (g + 1) * window),
                        0.0,
                        group[a],
                    )
                    for a in range(window)
                ]
                v = tn(jnp.concatenate(group, 0), jnp.concatenate(right, 0), precision)
                for i in range(first, count):
                    tiles[i] = jnp.where(inside, 0.0, tiles[i]) - v[8 * i : 8 * i + 8, :]
            group = []


class Mover:
    def __init__(self, send_sems, recv_sems):
        self.send_sems, self.recv_sems, self.used, self.sent = send_sems, recv_sems, 0, []

    def copy(self, src, dst, device):
        slot = self.used
        self.used += 1

        def build():
            return pltpu.make_async_remote_copy(
                src_ref=src(), dst_ref=dst(), send_sem=self.send_sems.at[slot],
                recv_sem=self.recv_sems.at[slot], device_id=device, device_id_type=MESH,
            )

        return build


def all_to_all_peers(mover, views, size, me, device, active=None):
    copies = [
        mover.copy(functools.partial(view, me), functools.partial(view, me), device(lax.rem(me + d, size)))
        for view in views
        for d in range(1, size)
    ]

    def start():
        for copy in copies:
            copy().start()

    def wait():
        for copy in copies:
            copy().wait_recv()

    def end():
        for copy in copies:
            copy().wait_send()

    def guarded(f):
        if active is None:
            return f
        return lambda: pl.when(active)(f)

    mover.sent.append(guarded(end))
    return guarded(start), guarded(wait)


def ring(mover, view, size, me, device, active=None):
    steps = []
    for hop in range(1, size // 2 + 1):
        copies = []
        for side, step in ((0, 1), (1, -1)):
            part = side if hop == size // 2 else None
            block = lax.rem(me - step * (hop - 1) + 2 * size, size)
            ref = functools.partial(view, block, part)
            copies.append(mover.copy(ref, ref, device(lax.rem(me + step + size, size))))

        def start(copies=copies):
            for copy in copies:
                copy().start()

        def wait(copies=copies):
            for copy in copies:
                copy().wait_recv()

        def end(copies=copies):
            for copy in copies:
                copy().wait_send()

        if active is not None:
            start, wait, end = (
                functools.partial(lambda f: pl.when(active)(f), f) for f in (start, wait, end)
            )
        mover.sent.append(end)
        steps.append((start, wait))
    return steps


def move_kernel(
    cov_ref, obs_ref, panel, rhs, cross, upper, inverses,
    lead, stage, work, row_ref, col_ref, send_sems, recv_sems, wide_sems, local_sems,
):
    p = lax.axis_index("prow")
    c = lax.axis_index("pcol")
    z, core = p // 2, lax.rem(p, 2)
    y, x = c // NX, lax.rem(c, NX)

    def at(zz, yy, xx, cc=core):
        return (2 * zz + cc, yy * NX + xx)

    def x_device(v):
        return at(z, y, v)

    def y_device(v):
        return at(z, v, x)

    def z_device(v):
        return at(v, y, x)

    sibling = at(z, y, x, 1 - core)

    barrier = pltpu.get_barrier_semaphore()

    def greet(device):
        pl.semaphore_signal(barrier, inc=1, device_id=device, device_id_type=MESH)

    for d in range(1, NY):
        greet(y_device(lax.rem(y + d, NY)))
    for d in range(1, NX):
        greet(x_device(lax.rem(x + d, NX)))
    for d in range(1, NZ):
        greet(z_device(lax.rem(z + d, NZ)))
    greet(sibling)
    for col in range(2):

        @pl.when(c == col)
        def _():
            @pl.loop(1, 32)
            def _(d):
                greet((p, lax.rem(c + d, 32)))

        @pl.when(c != col)
        def _():
            greet((p, col))

    others = NY + NX + NZ - 2
    pl.semaphore_wait(
        barrier,
        others + jnp.where(c != 0, 1, 0) + jnp.where(c != 1, 1, 0) + jnp.where(c <= 1, 31, 0),
    )

    mover = Mover(send_sems, recv_sems)

    def remote(src, dst, send, recv, device):
        return pltpu.make_async_remote_copy(
            src_ref=src, dst_ref=dst, send_sem=wide_sems.at[send], recv_sem=wide_sems.at[recv],
            device_id=device, device_id_type=MESH,
        )

    def local(src, dst, slot):
        return pltpu.make_async_copy(src, dst, local_sems.at[slot])

    def rows16(row, to):
        return cov_ref.at[row, to // NX, lax.rem(to, NX)]

    def lead_home(half, to):
        return stage if half else lead.at[core, to // NX, lax.rem(to, NX), :, 0:512]

    def piece(ref, part):
        rows = pl.ds(pl.multiple_of(8 * (part // 4), 8), 8)
        return ref.at[rows, pl.ds(pl.multiple_of(128 * lax.rem(part, 4), 128), 128)]

    def second(part, ys, xs):
        rows = pl.ds(pl.multiple_of(8 * (part // 4), 8), 8)
        lanes = pl.ds(pl.multiple_of(512 + 128 * lax.rem(part, 4), 128), 128)
        return lead.at[core, ys, xs, rows, lanes]

    def lead_share(half, to):
        dst = lead_home(half, to)
        return remote(rows16(0, to), dst, 2 * half, 2 * half + 1, (p, to))

    def lead_sender(half):
        return (c == half) & ((p == 0) if half == 0 else (z == 0))

    def lead_plane(half):
        return (p == 0) if half == 0 else (z == 0)

    def own_lead(half):
        return local(rows16(0, c), lead_home(half, c), half)

    def start_lead(half):
        @pl.when(lead_sender(half))
        def _():
            @pl.loop(1, 32)
            def _(d):
                lead_share(half, lax.rem(c + d, 32)).start()

            own_lead(half).start()

    def end_lead(half):
        @pl.when(lead_sender(half))
        def _():
            @pl.loop(1, 32)
            def _(d):
                lead_share(half, lax.rem(c + d, 32)).wait_send()

    def wait_lead(half):
        @pl.when(lead_plane(half) & (c != half))
        def _():
            lead_share(half, c).wait_recv()

        @pl.when(lead_sender(half))
        def _():
            own_lead(half).wait()

    def lead_down(half, to):
        if half:
            return remote(piece(stage, to), second(to, y, x), 6, 7, z_device(to))
        ref = lead_home(0, c)
        return remote(ref, ref, 4, 5, z_device(to))

    def own_piece():
        return local(stage.at[0:8, 0:128], lead.at[core, y, x, 0:8, 512:640], 6)

    def on_lead(half, condition):
        return (condition & (core == 0)) if half == 0 else condition

    def start_down(half):
        @pl.when(on_lead(half, z == 0))
        def _():
            @pl.loop(1, NZ)
            def _(d):
                lead_down(half, d).start()

            if half:
                own_piece().start()
                own_piece().wait()

    def wait_down(half):
        @pl.when(on_lead(half, z != 0))
        def _():
            lead_down(half, 0).wait_recv()

    def end_down(half):
        @pl.when(on_lead(half, z == 0))
        def _():
            @pl.loop(1, NZ)
            def _(d):
                lead_down(half, d).wait_send()

    def share_copy(col, to):
        dst = panel.at[0, to // NX, lax.rem(to, NX), :, 512 * col : 512 * col + 512]
        return remote(rows16(0, to), dst, 8, 9 + col, (p, to))

    def high_part(col, to):
        return panel.at[1, to, :, :, 512 * col : 512 * col + 512]

    def high_share(col, to):
        return remote(cov_ref.at[1, to], high_part(col, to), 15, 16 + col, y_device(to))

    def high_cast(col, to):
        return remote(high_part(col, y), high_part(col, y), 18, 19 + col, x_device(to))

    def slab_copy(to):
        return remote(cov_ref.at[0, to], cross.at[core, to], 11, 12, z_device(to))

    def rhs_copy(to):
        return remote(obs_ref.at[0], rhs.at[core, y, x], 13, 14, z_device(to))

    def own_high(col):
        return local(cov_ref.at[1, 0], high_part(col, 0), 5)

    def own_low(col):
        return local(rows16(0, c), panel.at[0, y, x, :, 512 * col : 512 * col + 512], 3)

    def own_rhs():
        return local(obs_ref.at[0], rhs.at[core, y, x], 2)

    def own_slab():
        return local(cov_ref.at[0, 0], cross.at[core, 0], 4)

    def both_columns(condition, action):
        for col in range(2):
            pl.when(condition(col))(functools.partial(action, col))

    start_lead(0)
    start_lead(1)

    def start_high(col):
        for d in range(1, NY):
            high_share(col, d).start()
        own_high(col).start()

    @pl.when(z == 0)
    def _():
        for d in range(1, NZ):
            rhs_copy(d).start()
        own_rhs().start()

    def start_low(col):
        @pl.loop(1, 32)
        def _(d):
            share_copy(col, lax.rem(c + d, 32)).start()

        own_low(col).start()

    def lead_y(half):
        return lambda block: lead.at[core, block, x, :, 512 * half : 512 * half + 512]

    def rhs_y(block):
        return rhs.at[core, block, x]

    def rhs_x(block):
        return rhs.at[core, :, block]

    def peers(views, size, me, device, active=None):
        return all_to_all_peers(mover, views, size, me, device, active)

    first_slots = mover.used
    mover.used += NY

    def first_y(d):
        ref = lead_y(0)(y)
        return pltpu.make_async_remote_copy(
            src_ref=ref, dst_ref=ref, send_sem=send_sems.at[first_slots + d],
            recv_sem=recv_sems.at[first_slots + y], device_id=y_device(lax.rem(y + d, NY)),
            device_id_type=MESH,
        )

    def first_y_wait(v):
        ref = lead_y(0)(v)
        return pltpu.make_async_remote_copy(
            src_ref=ref, dst_ref=ref, send_sem=send_sems.at[first_slots],
            recv_sem=recv_sems.at[first_slots + v], device_id=y_device(v), device_id_type=MESH,
        )

    def pair_rows(q, block):
        return lead.at[0, 2 * q : 2 * q + 2, block, :, 0:512]

    first_x = [
        [
            mover.copy(
                functools.partial(pair_rows, q, x), functools.partial(pair_rows, q, x),
                x_device(lax.rem(x + d, NX)),
            )
            for d in range(1, NX)
        ]
        for q in range(4)
    ]
    first_pair = [
        mover.copy(
            functools.partial(pair_rows, q, slice(0, NX)),
            functools.partial(pair_rows, q, slice(0, NX)), sibling,
        )
        for q in range(4)
    ]

    def y_arrived(q):
        @pl.when(core == 0)
        def _():
            for v in (2 * q, 2 * q + 1):

                @pl.when(y != v)
                def _():
                    first_y_wait(v).wait_recv()

            for copy in first_x[q]:
                copy().start()

    def x_arrived(q):
        @pl.when(core == 0)
        def _():
            for copy in first_x[q]:
                copy().wait_recv()
            first_pair[q]().start()

    def pair_arrived(q):
        @pl.when(core == 1)
        def _():
            first_pair[q]().wait_recv()

    def whole_or_half(view):
        return lambda block, part: view(
            slice(0, NY) if part is None else slice(4 * part, 4 * part + 4), block
        )

    second_y = peers([lambda block: second(z, block, x)], NY, y, y_device)
    second_x = peers([lambda block: second(z, slice(0, NY), block)], NX, x, x_device)
    second_z = ring(
        mover,
        lambda block, part: second(
            block, slice(0, NY) if part is None else slice(4 * part, 4 * part + 4), slice(0, NX)
        ),
        NZ, z, z_device,
    )
    rhs_gather = peers([rhs_y], NY, y, y_device)
    rhs_ring = ring(
        mover, whole_or_half(lambda rows, block: rhs.at[core, rows, block]), NX, x, x_device
    )
    cross_z = ring(
        mover,
        lambda block, part: (
            cross.at[core, block] if part is None else cross.at[core, block, 2 * part : 2 * part + 2]
        ),
        NZ, z, z_device,
    )
    low_rows = z // 2
    low_copies = [
        mover.copy(
            lambda: panel.at[0, y, x], lambda: panel.at[0, y, x], y_device(lax.rem(y + d, NY))
        )
        for d in range(1, NY)
    ]

    def low_y_start():
        for d, copy in enumerate(low_copies, 1):
            pl.when(lax.rem(y + d, NY) <= low_rows)(lambda copy=copy: copy().start())

    def low_y_end():
        for d, copy in enumerate(low_copies, 1):
            pl.when(lax.rem(y + d, NY) <= low_rows)(lambda copy=copy: copy().wait_send())

    mover.sent.append(low_y_end)

    def low_y_wait():
        @pl.when(y <= low_rows)
        def _():
            for copy in low_copies:
                copy().wait_recv()

    low_x = ring(
        mover,
        lambda block, part: panel.at[
            0, slice(0, NY) if part is None else slice(4 * part, 4 * part + 4), block
        ],
        NX, x, x_device, y <= low_rows,
    )
    high_y = ring(
        mover,
        lambda block, part: panel.at[
            1, block, slice(0, NX) if part is None else slice(2 * part, 2 * part + 2)
        ],
        NY, y, y_device,
    )

    def to_sibling(view):
        build = mover.copy(view, view, sibling)
        mover.sent.append(lambda: build().wait_send())
        return lambda: build().start(), lambda: build().wait_recv()

    second_pair = to_sibling(lambda: lead.at[core, :, :, :, 512:1024])
    rhs_pair = to_sibling(lambda: rhs.at[core])
    cross_pair = to_sibling(lambda: cross.at[core])

    wait_lead(0)
    start_down(0)
    wait_lead(1)
    start_down(1)
    @pl.when(z == 0)
    def _():
        for d in range(1, NZ):
            slab_copy(d).start()
        own_slab().start()

    def cast_high(col):
        @pl.when(y != 0)
        def _():
            high_share(col, y).wait_recv()

        @pl.when(y == 0)
        def _():
            own_high(col).wait()

        for d in range(1, NX):
            high_cast(col, lax.rem(x + d, NX)).start()

    def high_arrived():
        for col in range(2):

            @pl.when(x != col)
            def _():
                high_cast(col, col).wait_recv()

    def low_arrived():
        both_columns(lambda col: c != col, lambda col: share_copy(col, c).wait_recv())
        both_columns(lambda col: c == col, lambda col: own_low(col).wait())
        low_y_start()

    wait_down(0)

    @pl.when(core == 0)
    def _():
        for d in range(1, NY):
            first_y(d).start()

    both_columns(lambda col: c == col, start_high)

    wait_down(1)
    second_y[0]()
    y_arrived(0)
    y_arrived(1)
    second_y[1]()
    second_x[0]()
    y_arrived(2)
    y_arrived(3)
    both_columns(lambda col: c == col, start_low)
    second_x[1]()
    second_z[0][0]()
    x_arrived(0)
    x_arrived(1)
    both_columns(lambda col: x == col, cast_high)
    second_z[0][1]()
    second_z[1][0]()

    @pl.when(z != 0)
    def _():
        rhs_copy(0).wait_recv()
        slab_copy(0).wait_recv()

    @pl.when(z == 0)
    def _():
        own_rhs().wait()
        own_slab().wait()

    cross_z[0][0]()
    rhs_gather[0]()
    pair_arrived(0)

    def slot0():
        x_arrived(2)
        pair_arrived(1)
        second_z[1][1]()
        second_z[2][0]()
        cross_z[0][1]()
        cross_z[1][0]()
        low_arrived()

    def slot1():
        x_arrived(3)
        pair_arrived(2)
        second_z[2][1]()
        second_z[3][0]()
        high_arrived()
        high_y[0][0]()
        cross_z[1][1]()
        cross_z[2][0]()

    def slot2():
        pair_arrived(3)
        second_z[3][1]()
        second_pair[0]()
        high_y[0][1]()
        high_y[1][0]()
        low_y_wait()
        low_x[0][0]()
        cross_z[2][1]()
        cross_z[3][0]()
        rhs_gather[1]()

    def slot3():
        second_pair[1]()
        high_y[1][1]()
        high_y[2][0]()
        cross_z[3][1]()
        cross_pair[0]()
        rhs_ring[0][0]()

    def slot4():
        high_y[2][1]()
        high_y[3][0]()
        low_x[0][1]()
        low_x[1][0]()
        rhs_ring[0][1]()
        rhs_ring[1][0]()

    def slot5():
        rhs_ring[1][1]()
        rhs_pair[0]()

    def slot6():
        high_y[3][1]()
        low_x[1][1]()
        rhs_pair[1]()
        cross_pair[1]()

    slots = {0: slot0, 1: slot1, 2: slot2, 3: slot3, 4: slot4, 5: slot5, 6: slot6}

    upper[...] = jnp.zeros((1024, 1024), jnp.float32)

    @pl.loop(0, 8)
    def _(a):
        at_row = pl.ds(pl.multiple_of(128 * lax.rem(a, 4), 128), 128)
        at_wide = pl.ds(pl.multiple_of(512 * (a // 4), 512), 512)
        at_upper = pl.ds(pl.multiple_of(128 * a, 128), 128)

        @pl.when(a < 4)
        def _():
            for i in range(8):
                work[pl.ds(pl.multiple_of(128 * a + 16 * i, 16), 16), :] = lead[
                    0, 2 * a + i // NX, i % NX, :, 0:512
                ]

        @pl.when(a == 4)
        def _():
            for i in range(32):
                upper[16 * i : 16 * i + 16, 512:1024] = lead[0, i // NX, i % NX, :, 512:1024]
                work[16 * i : 16 * i + 16, :] = lead[1, i // NX, i % NX, :, 512:1024]
            for k in range(4):
                rows = slice(128 * k, 128 * k + 128)
                if k:
                    upper[rows, 512:1024] -= tn(
                        upper[0 : 128 * k, rows], upper[0 : 128 * k, 512:1024], HIGHEST
                    )
                upper[rows, 512:1024] = nn(inverses[k], upper[rows, 512:1024], HIGHEST)

            @pl.loop(0, 4)
            def _(i):
                cut = pl.ds(pl.multiple_of(128 * i, 128), 128)
                left = upper[0:512, pl.ds(pl.multiple_of(512 + 128 * i, 128), 128)]
                work[cut, :] -= tn(left, upper[0:512, 512:1024], HIGHEST)

        work[at_row, :] -= tn(upper[at_wide, at_upper], upper[at_wide, at_wide], HIGHEST)
        factor128(work[at_row, at_row], inverses.at[a], row_ref, col_ref)
        upper[at_upper, at_wide] = nn(inverses[a], work[at_row, :], HIGHEST)
        for index, events in slots.items():
            pl.when(a == index)(events)

    for end in mover.sent:
        end()

    @pl.when(core == 0)
    def _():
        for d in range(1, NY):
            first_y(d).wait_send()
        for q in range(4):
            for copy in first_x[q]:
                copy().wait_send()
            first_pair[q]().wait_send()

    end_lead(0)
    end_lead(1)
    end_down(0)
    end_down(1)
    for col in range(2):

        @pl.when(c == col)
        def _():
            @pl.loop(1, 32)
            def _(d):
                share_copy(col, lax.rem(c + d, 32)).wait_send()

            @pl.loop(1, NY)
            def _(d):
                high_share(col, d).wait_send()

        @pl.when(x == col)
        def _():
            for d in range(1, NX):
                high_cast(col, lax.rem(x + d, NX)).wait_send()

    @pl.when(z == 0)
    def _():
        @pl.loop(1, NZ)
        def _(d):
            rhs_copy(d).wait_send()
            slab_copy(d).wait_send()


def move(cov, obs):
    any_space = pl.BlockSpec(memory_space=pl.ANY)
    vmem = pl.BlockSpec(memory_space=pltpu.VMEM)
    return pl.pallas_call(
        move_kernel,
        out_shape=[
            jax.ShapeDtypeStruct((2, NY, NX, 16, 1024), jnp.float32),
            jax.ShapeDtypeStruct((2, NY, NX, 16, 256), jnp.float32),
            jax.ShapeDtypeStruct((2, NZ, 4, 16, 512), jnp.float32),
            jax.ShapeDtypeStruct((1024, 1024), jnp.float32),
            jax.ShapeDtypeStruct((8, 128, 128), jnp.float32),
        ],
        in_specs=[any_space] * 2,
        out_specs=[any_space] * 3 + [vmem] * 2,
        scratch_shapes=[
            pltpu.VMEM((2, NY, NX, 16, 1024), jnp.float32),
            pltpu.VMEM((16, 512), jnp.float32),
            pltpu.VMEM((512, 512), jnp.float32),
            pltpu.VMEM((128, 128), jnp.float32),
            pltpu.VMEM((128, 128), jnp.float32),
            pltpu.SemaphoreType.DMA((96,)),
            pltpu.SemaphoreType.DMA((96,)),
            pltpu.SemaphoreType.DMA((21,)),
            pltpu.SemaphoreType.DMA((7,)),
        ],
        compiler_params=pltpu.CompilerParams(
            collective_id=0, has_side_effects=True, vmem_limit_bytes=60 * 1024 * 1024
        ),
    )(cov, obs)


def update_kernel(
    upper_ref, inverses_ref, rhs_ref, cross_ref, panel_ref, cov_ref, obs_ref, out_ref, red_ref,
    u, inv, g, x, tile, flat, inv2, sems,
):
    p = lax.axis_index("prow")
    c = lax.axis_index("pcol")
    loads = [
        pltpu.make_async_copy(inverses_ref, inv, sems.at[0]),
        pltpu.make_async_copy(upper_ref, u, sems.at[1]),
        pltpu.make_async_copy(rhs_ref, g.at[:, 512:768], sems.at[2]),
        pltpu.make_async_copy(cross_ref, g.at[:, 0:512], sems.at[3]),
        pltpu.make_async_copy(panel_ref, x, sems.at[4]),
        pltpu.make_async_copy(cov_ref, tile, sems.at[5]),
    ]
    for load in loads:
        load.start()
    for load in loads[:2]:
        load.wait()
    for big in range(4):
        lo, mid, hi = 256 * big, 256 * big + 128, 256 * big + 256
        ia, ib = inv[2 * big], inv[2 * big + 1]
        inv2[big, 0:128, 0:128] = ia
        inv2[big, 0:128, 128:256] = jnp.zeros((128, 128), jnp.float32)
        inv2[big, 128:256, 0:128] = -nn(ib, tn(u[lo:mid, mid:hi], ia, HIGHEST), HIGHEST)
        inv2[big, 128:256, 128:256] = ib
    for load in loads[2:5]:
        load.wait()
    for big in range(4):
        lo, hi = 256 * big, 256 * big + 256
        g[lo:hi, :] = nn(inv2[big], g[lo:hi, :])
        for row in range(hi, 1024, 256):
            g[row : row + 256, :] -= tn(u[lo:hi, row : row + 256], g[lo:hi, :])

        for i in range(4):
            at = slice(256 * i, 256 * i + 256)
            solved = nt(x[at, lo:hi], inv2[big])
            x[at, lo:hi] = solved
            for start in range(hi, 1024, 256):
                x[at, start : start + 256] -= nn(solved, u[lo:hi, start : start + 256])

    loads[5].wait()
    sub = lax.broadcasted_iota(jnp.int32, (256, 512), 0)
    lane = lax.broadcasted_iota(jnp.int32, (256, 512), 1)

    def put(i, values):
        for row in range(32):
            for col in range(4):
                flat[pl.ds(1024 * i + 32 * row + col, 8, stride=4), :] = values[
                    8 * row : 8 * row + 8, 128 * col : 128 * col + 128
                ]

    for i in range(4):
        at = pl.ds(256 * i, 256)
        below = p + 16 * (i // 2)

        @pl.when(c <= 1)
        def _():
            half = jnp.where(c == 0, x[at, 0:512], x[at, 512:1024])
            row = sub + 256 * (i % 2)
            keep = (below > c) | ((below == c) & (row >= lane))
            put(i, jnp.where(keep, half, 0.0))

        @pl.when((c > 1) & (below >= c))
        def _():
            put(i, tile[at, :] - nn(x[at, :], g[:, 0:512]))

        @pl.when((c > 1) & (below < c))
        def _():
            flat[pl.ds(1024 * i, 1024), :] = jnp.zeros((1024, 128), jnp.float32)

    tile_out = pltpu.make_async_copy(flat, out_ref, sems.at[6])
    tile_out.start()
    solved_rhs = g[:, 512:768]
    low = x[pl.ds(pl.multiple_of(16 * c, 16), 16), :]
    high = x[pl.ds(pl.multiple_of(512 + 16 * c, 16), 16), :]
    red_ref[1] = obs_ref[1] - nn(high, solved_rhs)

    @pl.when(p > 1)
    def _():
        red_ref[0] = obs_ref[0] - nn(low, solved_rhs)

    @pl.when(p <= 1)
    def _():
        red_ref[0] = g[pl.ds(pl.multiple_of(512 * p + 16 * c, 16), 16), 512:768]

    tile_out.wait()


def update(upper, inverses, rhs, cross, panel, cov, obs):
    any_space = pl.BlockSpec(memory_space=pl.ANY)
    vmem = pl.BlockSpec(memory_space=pltpu.VMEM)
    return pl.pallas_call(
        update_kernel,
        out_shape=[
            jax.ShapeDtypeStruct((4096, 128), jnp.float32),
            jax.ShapeDtypeStruct((2, 16, 256), jnp.float32),
        ],
        in_specs=[any_space] * 6 + [vmem],
        out_specs=[any_space, vmem],
        scratch_shapes=[
            pltpu.VMEM((1024, 1024), jnp.float32),
            pltpu.VMEM((8, 128, 128), jnp.float32),
            pltpu.VMEM((1024, 768), jnp.float32),
            pltpu.VMEM((1024, 1024), jnp.float32),
            pltpu.VMEM((1024, 512), jnp.float32),
            pltpu.VMEM((4096, 128), jnp.float32),
            pltpu.VMEM((4, 256, 256), jnp.float32),
            pltpu.SemaphoreType.DMA((7,)),
        ],
        compiler_params=pltpu.CompilerParams(vmem_limit_bytes=60 * 1024 * 1024),
    )(upper, inverses, rhs, cross, panel, cov, obs)


def body(covariance, observations):
    cov = covariance.reshape(2, 512, 512)
    obs = observations.reshape(2, 16, 256)
    panel, rhs, cross, upper, inverses = move(cov.reshape(2, NY, NX, 16, 512), obs)
    factor, reduced = update(
        upper, inverses, rhs.reshape(1024, 256), cross.reshape(1024, 512),
        panel.reshape(1024, 1024), cov.reshape(1024, 512), obs,
    )
    return factor.reshape(covariance.shape), reduced.reshape(observations.shape)


def solution(mesh):
    return jax.shard_map(
        body,
        mesh=mesh,
        in_specs=(P(None, "prow", None, None, "pcol", None), P(None, "prow", "pcol", None)),
        out_specs=(P(None, "prow", None, None, "pcol", None), P(None, "prow", "pcol", None)),
        check_vma=False,
    )
```
